256 devices in a mesh: gx: 16 (over x, z_lo, core), gy: 16 (over y, z_hi).
Axes of the slice: x: 4, y: 4, z: 8 (z_hi: 4, z_lo: 2; z = z_hi * 2 + z_lo), core: 2. Of those that a mesh axis runs over, the one named last changes fastest.
Arguments:
- positions: float32 [3, 32, 32, 4, 128], P(None, 'gx', 'gy'), may hold values from 0 to 64, as said below
- velocity: float32 [3, 32, 32, 4, 128], P(None, 'gx', 'gy'), may hold values from -4 to 4
- density: float32 [32, 32, 4, 128], P('gx', 'gy'), may hold values from 0.8 to 1.2
- mass: float32 [32, 32, 4, 128], P('gx', 'gy'), may hold values from 0.05 to 0.15
- kind: int32 [32, 32, 4, 128], P('gx', 'gy'), may hold values from 0 to 2, as said below
Outputs:
- density_rate: float32 [32, 32, 4, 128], P('gx', 'gy')
- acceleration: float32 [3, 32, 32, 4, 128], P(None, 'gx', 'gy')
The draws below stay inside these ranges and needn't reach their ends.
Inputs may be any that keep to these rules, and one draw needn't show every extreme that they name: `kind`: in every cell the particles fill the first slots and the rest are empty (0); each cell holds at least 32 particles; particles in the lowest layer of cells (third index 0) are boundary particles (2), all others fluid (1). positions[:, i, j, k, s] lies in the cube of side 2 whose lowest corner is 2 * (i, j, k).
All inputs are finite; a program needn't handle non-finite values.
Results may differ from the reference program's by a relative error of at most 0.000036.
Values sent between devices are 32-bit elements; how exact they have to be, the bound alone decides.
A program may use at most 192 MiB of HBM per device.

```python
import math
import jax
import jax.numpy as jnp
from jax import lax

CZ = 4
S = 128
NX = 32
NY = 32


def draw_positions(key, part):
    key = jax.random.fold_in(key, 11)
    spot = jax.random.uniform(key, (3, NX, NY, CZ, S), jnp.float32)
    shape = (NX, NY, CZ, S)
    corner = jnp.stack([lax.broadcasted_iota(jnp.float32, shape, 0), lax.broadcasted_iota(jnp.float32, shape, 1), lax.broadcasted_iota(jnp.float32, shape, 2)])
    return (2.0 * (corner + spot)).astype(jnp.float32)


def draw_kind(key, part):
    key = jax.random.fold_in(key, 23)
    counts = jax.random.randint(key, (NX, NY, CZ, 1), S // 4, S + 1)
    slot = lax.broadcasted_iota(jnp.int32, (NX, NY, CZ, S), 3)
    level = lax.broadcasted_iota(jnp.int32, (NX, NY, CZ, S), 2)
    return jnp.where(slot < counts, jnp.where(level == 0, 2, 1), 0).astype(jnp.int32)


def steps_of(own_key, extent, pieces, low, top_value):
    def one(axis_at, shards_of):
        heights = jax.random.uniform(jax.random.fold_in(jax.random.fold_in(own_key, 6), axis_at), (shards_of,), jnp.float32, low / len(pieces), top_value / len(pieces))
        return jnp.repeat(jnp.exp(heights), extent[axis_at] // shards_of).reshape((-1,) + (1,) * (len(extent) - axis_at - 1))

    factor_of = one(*pieces[0])
    for cut in pieces[1:]:
        factor_of = factor_of * one(*cut)
    return factor_of


def scatter_about(key, dims, scale, reach, split=(), kind=jnp.bfloat16):
    level = steps_of(key, dims, split, -0.22, 0.18) if split else 1.0
    array = jax.random.normal(key, dims, jnp.float32) * scale * level
    return jnp.minimum(jnp.maximum(array, -reach), reach).astype(kind)


def setup_inputs(seed: int = 0) -> dict:
    keys = jax.random.split(jax.random.key(seed), 6)
    return {
        "positions": draw_positions(jax.random.fold_in(keys[5], 71), 0),
        "velocity": scatter_about(keys[1], (3, NX, NY, CZ, S), 1.0, 4.0, ((1, 16), (2, 16)), jnp.float32),
        "density": jnp.clip(0.8 + 0.40000004 * jax.random.uniform(keys[2], (NX, NY, CZ, S), jnp.float32) ** steps_of(keys[2], (NX, NY, CZ, S), ((0, 16), (1, 16)), -0.2, 0.2), 0.8, 1.2),
        "mass": jnp.clip(0.05 + 0.10000001 * jax.random.uniform(keys[3], (NX, NY, CZ, S), jnp.float32) ** steps_of(keys[3], (NX, NY, CZ, S), ((0, 16), (1, 16)), -0.2, 0.2), 0.05, 0.15),
        "kind": draw_kind(jax.random.fold_in(keys[5], 71), 0),
    }


KERNEL_NORM = 21.0 / (16.0 * math.pi)
SOUND = 3.0
STIFF = SOUND * SOUND / 7.0
DELTA = 0.1
ALPHA = 0.1
SOFTEN = 0.01
FLOOR = 0.25
GRAVITY = 1.0
OFFSETS = [(a, b, c) for a in (-1, 0, 1) for b in (-1, 0, 1) for c in (-1, 0, 1)]
MOMENT_PAIRS = [(0, 0), (0, 1), (0, 2), (1, 1), (1, 2), (2, 2)]

def pressure(values):
    return STIFF * (values ** 7 - 1.0)

def pair_geometry(target, source):
    sep = target[0:3, ..., :, None] - source[0:3, ..., None, :]
    dist2 = sep[0] * sep[0] + sep[1] * sep[1] + sep[2] * sep[2]
    wedge = jnp.maximum(1.0 - 0.5 * jnp.sqrt(dist2), 0.0)
    coef = source[7][..., None, :] * (-5.0 * KERNEL_NORM) * wedge * wedge * wedge
    return (sep, dist2, coef)

def first_terms(target, source):
    sep, dist2, coef = pair_geometry(target, source)
    jump = (source[6][..., None, :] - target[6][..., :, None]) * coef
    moments = [-lax.optimization_barrier(jnp.sum(coef * sep[a] * sep[b], axis=-1)) for a, b in MOMENT_PAIRS]
    slopes = [lax.optimization_barrier(jnp.sum(jump * sep[a], axis=-1)) for a in range(3)]
    return jnp.stack(moments + slopes)

def second_terms(target, source):
    sep, dist2, coef = pair_geometry(target, source)
    rho_target = target[6][..., :, None]
    rho_source = source[6][..., None, :]
    dvel = source[3:6, ..., None, :] - target[3:6, ..., :, None]
    vdot = dvel[0] * sep[0] + dvel[1] * sep[1] + dvel[2] * sep[2]
    gsep = (target[8][..., :, None] + source[8][..., None, :]) * sep[0]
    gsep = gsep + (target[9][..., :, None] + source[9][..., None, :]) * sep[1]
    gsep = gsep + (target[10][..., :, None] + source[10][..., None, :]) * sep[2]
    inverse = 1.0 / (dist2 + SOFTEN)
    flow = lax.optimization_barrier(jnp.sum(coef * vdot, axis=-1))
    spread = lax.optimization_barrier(jnp.sum(coef * (-2.0 * (rho_source - rho_target) * dist2 * inverse - gsep), axis=-1))
    push = (-(target[11][..., :, None] + source[11][..., None, :]) - ALPHA * SOUND * vdot * inverse) * coef
    forces = [lax.optimization_barrier(jnp.sum(push * sep[a], axis=-1)) for a in range(3)]
    return jnp.stack([flow, spread] + forces)

def sweep(padded, terms, count):
    width_a = padded.shape[1] - 2
    width_b = padded.shape[2] - 2
    layers = padded.shape[3]
    slots = padded.shape[4]
    shifted = jnp.pad(padded, ((0, 0), (0, 0), (0, 0), (1, 1), (0, 0)))

    def layer(level, result):
        block = lax.dynamic_slice_in_dim(shifted, level, 3, axis=3)
        target = block[:, 1:1 + width_a, 1:1 + width_b, 1]
        total = jnp.zeros((count, width_a, width_b, slots), jnp.float32)
        for step_a, step_b, step_c in OFFSETS:
            source = block[:, 1 + step_a:1 + step_a + width_a, 1 + step_b:1 + step_b + width_b, 1 + step_c]
            total = total + terms(target, source)
        return lax.dynamic_update_index_in_dim(result, total, level, 3)
    start = jnp.zeros((count, width_a, width_b, layers, slots), jnp.float32)
    return lax.fori_loop(0, layers, layer, start)

def renormalized(sums):
    m00 = sums[0] + FLOOR
    m01 = sums[1]
    m02 = sums[2]
    m11 = sums[3] + FLOOR
    m12 = sums[4]
    m22 = sums[5] + FLOOR
    c00 = m11 * m22 - m12 * m12
    c01 = m02 * m12 - m01 * m22
    c02 = m01 * m12 - m02 * m11
    c11 = m00 * m22 - m02 * m02
    c12 = m01 * m02 - m00 * m12
    c22 = m00 * m11 - m01 * m01
    det = m00 * c00 + m01 * c01 + m02 * c02
    g0 = sums[6]
    g1 = sums[7]
    g2 = sums[8]
    return jnp.stack([(c00 * g0 + c01 * g1 + c02 * g2) / det, (c01 * g0 + c11 * g1 + c12 * g2) / det, (c02 * g0 + c12 * g1 + c22 * g2) / det])

def finish(state, rates, kind):
    rho = state[6]
    rate = -rho * rates[0] + DELTA * SOUND * rates[1]
    accel = jnp.stack([rates[2] / rho, rates[3] / rho, rates[4] / rho - GRAVITY])
    rate = jnp.where(kind > 0, rate, 0.0)
    accel = jnp.where((kind == 1)[None], accel, 0.0)
    return (rate, accel)

def reference(positions, velocity, density, mass, kind):
    volume = jnp.where(kind > 0, mass, 0.0) / density
    state = jnp.concatenate([positions, velocity, density[None], volume[None]], axis=0)
    padded = jnp.pad(state, ((0, 0), (1, 1), (1, 1), (0, 0), (0, 0)))
    gradient = renormalized(sweep(padded, first_terms, 9))
    gradient_pad = jnp.pad(gradient, ((0, 0), (1, 1), (1, 1), (0, 0), (0, 0)))
    combined = jnp.concatenate([padded, gradient_pad, pressure(padded[6])[None]], axis=0)
    rates = sweep(combined, second_terms, 5)
    return finish(state, rates, kind)
```

```python
import functools
import math

import jax
import jax.numpy as jnp
from jax import lax
from jax.experimental import pallas as pl
from jax.experimental.pallas import tpu as pltpu
from jax.sharding import PartitionSpec as P

MESH = pl.DeviceIdType.MESH
KERNEL_NORM = 21.0 / (16.0 * math.pi)
SCALE = -5.0 * KERNEL_NORM
STIFF = 9.0 / 7.0
DELTA_SOUND = 0.3
ALPHA_SOUND = 0.3
FLOOR = 0.25
GRAVITY = 1.0
SOFT4 = 0.0025

F32 = jnp.float32
BF16 = jnp.bfloat16
RAW = 80
SIDES = [(i, j) for i in (-1, 0, 1) for j in (-1, 0, 1) if (i, j) != (0, 0)]
TINY = 1e-12
HALVES = {0: ((0, 256), (0, 256), (128, 128)), 1: ((0, 128), (0, 256), (0, 256))}


def pieces(x):
    a = x.astype(BF16).astype(F32)
    r = x - a
    b = r.astype(BF16).astype(F32)
    return a, b, r - b


def power7(r):
    r2 = r * r
    r4 = r2 * r2
    return STIFF * (r4 * r2 * r - 1.0)


def distance_rows(xs, source):
    half = [0.5 * x for x in xs]
    cut = [pieces(h) for h in half]
    norm = pieces(half[0] * half[0] + half[1] * half[1] + half[2] * half[2])
    one = jnp.ones_like(half[0])
    rows = []
    for i in range(3):
        for j in range(3 - i):
            for d in range(3):
                rows.append(-2.0 * cut[d][i] if source else cut[d][j])
    rows += list(norm) + [one] * 3 if source else [one] * 3 + list(norm)
    return rows


def kernel(comm, pos_ref, vel_ref, rho_ref, mass_ref, kind_ref, rate_ref, acc_ref,
           ext, gext, raw, traw, feat_c, feat_d, feat_g, far, near, chl, dhl, sums, parts, mask,
           send_sem, recv_sem, gsend_sem, grecv_sem):
    if comm:
        gx = lax.axis_index("gx")
        gy = lax.axis_index("gy")
        nx = lax.axis_size("gx")
        ny = lax.axis_size("gy")
    else:
        gx, gy, nx, ny = jnp.int32(1), jnp.int32(1), 16, 16

    def peer(i, j):
        return (lax.rem(gx + i + nx, nx), lax.rem(gy + j + ny, ny))

    if comm:
        barrier = pltpu.get_barrier_semaphore()
        for i, j in SIDES:
            pl.semaphore_signal(barrier, inc=1, device_id=peer(i, j), device_id_type=MESH)

    kind = kind_ref[...]
    rho = rho_ref[...]
    vol = jnp.where(kind > 0, mass_ref[...], 0.0) / rho * SCALE
    own = [pos_ref[0], pos_ref[1], pos_ref[2], vel_ref[0], vel_ref[1], vel_ref[2], rho - 1.0, vol]

    def place(buf, rows, values):
        for a in range(2):
            for b in range(2):
                base = ((a + 1) * 4 + b + 1) * rows
                for ch, value in enumerate(values):
                    at = (a * 2 + b) * 4
                    buf[base + ch * 4:base + ch * 4 + 4, :] = value[at:at + 4, :]

    place(ext, 32, own)

    def swap(buf, rows, ssem, rsem):
        copies = []
        n = 0
        for i, j in SIDES:
            avals = (0, 1) if i == 0 else ((1,) if i == 1 else (0,))
            bvals = (0, 1) if j == 0 else ((1,) if j == 1 else (0,))
            runs = []
            for a in avals:
                src = (a + 1) * 4 + bvals[0] + 1
                dst = (a + 1 - 2 * i) * 4 + bvals[0] + 1 - 2 * j
                runs.append((src, dst, len(bvals)))
            for src, dst, count in runs:
                copies.append(pltpu.make_async_remote_copy(
                    src_ref=buf.at[pl.ds(src * rows, count * rows)],
                    dst_ref=buf.at[pl.ds(dst * rows, count * rows)],
                    send_sem=ssem.at[n], recv_sem=rsem.at[n],
                    device_id=peer(i, j), device_id_type=MESH))
                n += 1
        return copies

    if comm:
        pl.semaphore_wait(barrier, 8)
        moves = swap(ext, 32, send_sem, recv_sem)
        for c in moves:
            c.start()

    row = lax.broadcasted_iota(jnp.int32, (16, 128), 0)
    upper = lax.rem(row, 4) >= 2
    ox = ((gx * 2 + 1) * 2).astype(F32)
    oy = ((gy * 2 + 1) * 2).astype(F32)
    xt = [own[0] - ox, own[1] - oy, own[2] - jnp.where(upper, 6.0, 2.0)]
    for k, value in enumerate(distance_rows(xt, False)):
        for h in range(2):
            traw[pl.ds(h * 8 * 24 + k, 8, stride=24), :] = value[h * 8:h * 8 + 8]
    zeros = jnp.zeros((128, 256), BF16)
    for t in range(8):
        near[t] = zeros
        both = jnp.concatenate([traw[(2 * t + h) * 24:(2 * t + h + 1) * 24, :] for h in range(2)], axis=1)
        near[t, 0:32, :] = jnp.concatenate([both, jnp.zeros((8, 256), F32)], axis=0).astype(BF16)

    if comm:
        for c in moves:
            c.wait()

    col = lax.broadcasted_iota(jnp.int32, (16, 128), 0)
    ca = col // 4
    cb = lax.rem(col, 4)
    inside = ((ca > 0) | (gx > 0)) & ((ca < 3) | (gx < nx - 1)) & ((cb > 0) | (gy > 0)) & ((cb < 3) | (gy < ny - 1))

    def chan(ch, layer):
        return ext[pl.ds(ch * 4 + layer, 16, stride=32), :]

    def put(buf, rows, p, l, f, value):
        for h in range(2):
            buf[pl.ds(((p * 16 + 8 * h) * 3 + l) * rows + f, 8, stride=3 * rows), :] = value[8 * h:8 * h + 8]

    for p in range(2):
        for l in range(3):
            layer = p + l
            x = [chan(0, layer) - ox, chan(1, layer) - oy, chan(2, layer) - (6.0 if p else 2.0)]
            v = [chan(3 + d, layer) for d in range(3)]
            r = chan(6, layer)
            w = jnp.where(inside, chan(7, layer), 0.0)
            pr = power7(r + 1.0)
            vx = v[0] * x[0] + v[1] * x[1] + v[2] * x[2]
            wx = [w * x[d] for d in range(3)]
            wxx = [wx[a] * x[b] for a in range(3) for b in range(a, 3)]
            wv = [w * v[d] for d in range(3)]
            wr = w * r
            wp = w * pr
            rows_c = [w] + wx + wxx + [wr] + [wr * x[d] for d in range(3)] + wv + [w * vx] + [wp] + [wp * x[d] for d in range(3)]
            zero = jnp.zeros_like(w)
            rows_c += [zero, zero]
            e = [pieces(w), pieces(wr)]
            rows_d = wv + wx + wxx + [wv[a] * x[b] for a in range(3) for b in range(3)] + [w * vx * x[d] for d in range(3)]
            rows_d += [e[0][0], e[1][0], e[0][1], e[1][1], e[0][2], e[1][2], zero, zero]
            rows = rows_c + rows_d + distance_rows(x, True)
            for f, value in enumerate(rows):
                put(raw, RAW, p, l, f, value)

    eye = (lax.broadcasted_iota(jnp.int32, (128, 128), 0) == lax.broadcasted_iota(jnp.int32, (128, 128), 1))
    eye16 = jnp.where(eye, 1.0, 0.0).astype(BF16)
    mask[0] = jnp.ones((128, 128), F32)
    mask[1] = jnp.where(eye, 0.0, 1.0)
    mask[2] = jnp.ones((128, 128), F32)

    @pl.loop(0, 96)
    def _(n):
        base = pl.multiple_of(n * RAW, 8)
        got = raw[pl.ds(base, RAW), :]
        c3 = pieces(got[0:24])
        feat_c[n] = jnp.concatenate(list(c3) + [jnp.zeros((8, 128), F32)], axis=0).astype(BF16)
        d3 = pieces(got[24:48])
        feat_d[n] = jnp.concatenate(list(d3) + [got[48:56]], axis=0).astype(BF16)
        dist = jnp.concatenate([got[56:80], jnp.zeros((104, 128), F32)], axis=0).astype(BF16)
        far[n] = lax.dot_general(eye16, dist, (((1,), (1,)), ((), ())), preferred_element_type=F32).astype(BF16)

    for t in range(8):
        sums[t] = jnp.zeros((160, 256), F32)
    for q in range(36):
        chl[q, 0, 512:768, 0:128] = jnp.zeros((256, 128), BF16)
        chl[q, 1, 0:256, 128:256] = jnp.zeros((256, 128), BF16)
    for db in range(3):
        dhl[0, db, 512:768, 0:128] = jnp.zeros((256, 128), BF16)
        dhl[1, db, 0:256, 128:256] = jnp.zeros((256, 128), BF16)

    def two(x):
        hi = x.astype(BF16)
        lo = (x - hi.astype(F32)).astype(BF16)
        return hi, lo

    @pl.loop(0, 12)
    def _(n):
        tc = n // 3
        da = lax.rem(n, 3)
        ta = tc // 2
        tb = lax.rem(tc, 2)
        for p in range(2):
            nt = near[tc * 2 + p]
            fc = []
            fd = []
            for db in range(3):
                col = (ta + da) * 4 + tb + db
                cell0 = (p * 16 + col) * 3
                q = n * 3 + db
                for l in range(3):
                    lane, width = HALVES[p][l]
                    d2 = jnp.dot(far[cell0 + l], nt[:, lane:lane + width], preferred_element_type=F32)
                    d2 = jnp.maximum(d2, TINY)
                    wedge = jnp.maximum(1.0 - d2 * lax.rsqrt(d2), 0.0)
                    c = wedge * wedge * wedge
                    d = c * pl.reciprocal(d2 + SOFT4, approx=True)
                    if db == 1 and l - p in (0, 1):
                        halves = [d[:, 0:128], d[:, 128:256]]
                        halves[l - p] = halves[l - p] * mask[da]
                        d = jnp.concatenate(halves, axis=1)
                    chi, clo = two(c)
                    chl[q, p, l * 256:l * 256 + 128, lane:lane + width] = chi
                    chl[q, p, l * 256 + 128:l * 256 + 256, lane:lane + width] = clo
                    dhi, dlo = two(d)
                    dhl[p, db, l * 256:l * 256 + 128, lane:lane + width] = dhi
                    dhl[p, db, l * 256 + 128:l * 256 + 256, lane:lane + width] = dlo
                    fc += [feat_c[cell0 + l]] * 2
                    fd += [feat_d[cell0 + l]] * 2
            lhs_c = jnp.concatenate(fc, axis=1)
            lhs_d = jnp.concatenate(fd, axis=1)
            rc = chl[pl.ds(n * 3, 3), p].reshape(2304, 256)
            rd = dhl[p].reshape(2304, 256)
            t = tc * 2 + p
            sums[t, 0:80, :] += jnp.dot(lhs_c, rc, preferred_element_type=F32)
            sums[t, 80:160, :] += jnp.dot(lhs_d, rd, preferred_element_type=F32)

    for t in range(8):
        for h in range(2):
            s = sums[t, :, h * 128:h * 128 + 128]
            base = (2 * t + h) * 56
            parts[base:base + 24, :] = s[0:24] + s[24:48] + s[48:72]
            parts[base + 24:base + 48, :] = s[80:104] + s[104:128] + s[128:152]
            parts[base + 48:base + 56, :] = s[152:160]

    def part(f, stride=56):
        return jnp.concatenate([parts[pl.ds(h * 8 * stride + f, 8, stride=stride), :] for h in range(2)], axis=0)

    def dot3(a, b):
        return a[0] * b[0] + a[1] * b[1] + a[2] * b[2]

    pc = [part(f) for f in range(22)]
    s0, s1, sr, srx, sv, svx, sp, spx = pc[0], pc[1:4], pc[10], pc[11:14], pc[14:17], pc[17], pc[18], pc[19:22]
    pair = {}
    n = 0
    for a in range(3):
        for b in range(a, 3):
            pair[a, b] = pair[b, a] = n
            n += 1
    mom = {}
    for a in range(3):
        for b in range(a, 3):
            m = -(pc[4 + pair[a, b]] - xt[a] * s1[b] - xt[b] * (s1[a] - xt[a] * s0))
            mom[a, b] = m + FLOOR if a == b else m
    rt = own[6]
    back = [s0 * xt[a] - s1[a] for a in range(3)]
    slope = [(sr * xt[a] - srx[a]) - rt * back[a] for a in range(3)]
    m00, m01, m02, m11, m12, m22 = mom[0, 0], mom[0, 1], mom[0, 2], mom[1, 1], mom[1, 2], mom[2, 2]
    c00 = m11 * m22 - m12 * m12
    c01 = m02 * m12 - m01 * m22
    c02 = m01 * m12 - m02 * m11
    c11 = m00 * m22 - m02 * m02
    c12 = m01 * m02 - m00 * m12
    c22 = m00 * m11 - m01 * m01
    det = m00 * c00 + m01 * c01 + m02 * c02
    grad = [(c00 * slope[0] + c01 * slope[1] + c02 * slope[2]) / det,
            (c01 * slope[0] + c11 * slope[1] + c12 * slope[2]) / det,
            (c02 * slope[0] + c12 * slope[1] + c22 * slope[2]) / det]

    place(gext, 16, grad)
    if comm:
        moves = swap(gext, 16, gsend_sem, grecv_sem)
        for c in moves:
            c.start()

    vt = own[3:6]
    pt = power7(rho)
    vtx = dot3(vt, xt)
    flow = dot3(sv, xt) - svx - vtx * s0 + dot3(vt, s1)
    pd = [part(24 + f) for f in range(30)]
    d0 = pd[24] + pd[26] + pd[28]
    dr = pd[25] + pd[27] + pd[29]
    dv, d1, dxx, dvx, dvxx = pd[0:3], pd[3:6], pd[6:12], [pd[12:15], pd[15:18], pd[18:21]], pd[21:24]
    spread = -2.0 * ((sr - rt * s0) - SOFT4 * (dr - rt * d0))
    trace = dvx[0][0] + dvx[1][1] + dvx[2][2]
    head = dot3(dv, xt) - trace - vtx * d0 + dot3(vt, d1)
    push = []
    for b in range(3):
        tail = (xt[0] * dvx[0][b] + xt[1] * dvx[1][b] + xt[2] * dvx[2][b] - dvxx[b] - vtx * d1[b]
                + vt[0] * dxx[pair[0, b]] + vt[1] * dxx[pair[1, b]] + vt[2] * dxx[pair[2, b]])
        push.append(-(pt * back[b] + (sp * xt[b] - spx[b])) - (0.25 * ALPHA_SOUND) * (xt[b] * head - tail))
    moving = kind == 1
    for b in range(3):
        force = push[b] / rho - (GRAVITY if b == 2 else 0.0)
        acc_ref[b] = jnp.where(moving, force, 0.0)
    spread = spread - dot3(grad, back)

    if comm:
        for c in moves:
            c.wait()

    for p in range(2):
        for l in range(3):
            layer = p + l
            x = [chan(0, layer) - ox, chan(1, layer) - oy, chan(2, layer) - (6.0 if p else 2.0)]
            w = jnp.where(inside, chan(7, layer), 0.0)
            g = [gext[pl.ds(d * 4 + layer, 16, stride=16), :] for d in range(3)]
            rows = [pieces(w * g[d]) for d in range(3)] + [pieces(w * dot3(g, x))]
            for k in range(3):
                for f in range(4):
                    put(raw, 16, p, l, k * 4 + f, rows[f][k])
            for f in range(12, 16):
                put(raw, 16, p, l, f, jnp.zeros_like(w))

    @pl.loop(0, 96)
    def _(n):
        feat_g[n] = raw[pl.ds(pl.multiple_of(n * 16, 16), 16), :].astype(BF16)

    for t in range(8):
        tc, p = t // 2, t % 2
        ta, tb = tc // 2, tc % 2
        fg = []
        for da in range(3):
            for db in range(3):
                for l in range(3):
                    fg += [feat_g[(p * 16 + (ta + da) * 4 + tb + db) * 3 + l]] * 2
        rc = chl[tc * 9:tc * 9 + 9, p].reshape(6912, 256)
        s = jnp.dot(jnp.concatenate(fg, axis=1), rc, preferred_element_type=F32)
        for h in range(2):
            parts[(2 * t + h) * 16:(2 * t + h + 1) * 16, :] = s[:, h * 128:h * 128 + 128]
    q = [part(f, 16) for f in range(12)]
    q = [q[f] + q[f + 4] + q[f + 8] for f in range(4)]
    spread = spread - (dot3(q, xt) - q[3])
    rate = -rho * flow + DELTA_SOUND * spread
    rate_ref[...] = jnp.where(kind > 0, rate, 0.0)


def local(comm, positions, velocity, density, mass, kind):
    vmem = pl.BlockSpec(memory_space=pltpu.VMEM)
    dma = pltpu.SemaphoreType.DMA
    rate, acc = pl.pallas_call(
        functools.partial(kernel, comm),
        out_shape=(jax.ShapeDtypeStruct((16, 128), F32), jax.ShapeDtypeStruct((3, 16, 128), F32)),
        in_specs=[vmem] * 5,
        out_specs=(vmem, vmem),
        scratch_shapes=[
            pltpu.VMEM((512, 128), F32),
            pltpu.VMEM((256, 128), F32),
            pltpu.VMEM((96 * RAW, 128), F32),
            pltpu.VMEM((16 * 24, 128), F32),
            pltpu.VMEM((96, 80, 128), BF16),
            pltpu.VMEM((96, 80, 128), BF16),
            pltpu.VMEM((96, 16, 128), BF16),
            pltpu.VMEM((96, 128, 128), BF16),
            pltpu.VMEM((8, 128, 256), BF16),
            pltpu.VMEM((36, 2, 768, 256), BF16),
            pltpu.VMEM((2, 3, 768, 256), BF16),
            pltpu.VMEM((8, 160, 256), F32),
            pltpu.VMEM((16 * 56, 128), F32),
            pltpu.VMEM((3, 128, 128), F32),
            dma((10,)), dma((10,)), dma((10,)), dma((10,)),
        ],
        compiler_params=pltpu.CompilerParams(
            vmem_limit_bytes=56 * 1024 * 1024,
            **(dict(collective_id=0, has_side_effects=True) if comm else {})),
        cost_estimate=pl.CostEstimate(flops=2 * 10**9, bytes_accessed=10**6, transcendentals=10**7),
    )(positions.reshape(3, 16, 128), velocity.reshape(3, 16, 128), density.reshape(16, 128),
      mass.reshape(16, 128), kind.reshape(16, 128))
    return rate.reshape(2, 2, 4, 128), acc.reshape(3, 2, 2, 4, 128)


def solution(mesh):
    in_specs = (
        P(None, "gx", "gy", None, None),
        P(None, "gx", "gy", None, None),
        P("gx", "gy", None, None),
        P("gx", "gy", None, None),
        P("gx", "gy", None, None),
    )
    out_specs = (P("gx", "gy", None, None), P(None, "gx", "gy", None, None))
    return jax.shard_map(functools.partial(local, True), mesh=mesh, in_specs=in_specs, out_specs=out_specs,
                         check_vma=False)
```

```python
import functools
import math

import jax
import jax.numpy as jnp
from jax import lax
from jax.experimental import pallas as pl
from jax.experimental.pallas import tpu as pltpu
from jax.sharding import PartitionSpec as P

MESH = pl.DeviceIdType.MESH
KERNEL_NORM = 21.0 / (16.0 * math.pi)
SCALE = -5.0 * KERNEL_NORM
STIFF = 9.0 / 7.0
DELTA_SOUND = 0.3
ALPHA_SOUND = 0.3
FLOOR = 0.25
GRAVITY = 1.0
SOFT4 = 0.0025

F32 = jnp.float32
BF16 = jnp.bfloat16
RAW = 80
SIDES = [(i, j) for i in (-1, 0, 1) for j in (-1, 0, 1) if (i, j) != (0, 0)]
TINY = 1e-12
BOTH = {0: (0, 1), 1: (2, 3)}
ONE = {0: 2, 1: 1}
LANE = {0: 128, 1: 0}
CUT = 1


def pieces(x):
    a = x.astype(BF16).astype(F32)
    r = x - a
    b = r.astype(BF16).astype(F32)
    return a, b, r - b


def power7(r):
    r2 = r * r
    r4 = r2 * r2
    return STIFF * (r4 * r2 * r - 1.0)


def distance_rows(xs, source):
    half = [0.5 * x for x in xs]
    cut = [pieces(h) for h in half]
    norm = pieces(half[0] * half[0] + half[1] * half[1] + half[2] * half[2])
    one = jnp.ones_like(half[0])
    rows = []
    for i in range(3):
        for j in range(3 - i):
            for d in range(3):
                rows.append(-2.0 * cut[d][i] if source else cut[d][j])
    rows += list(norm) + [one] * 3 if source else [one] * 3 + list(norm)
    return rows


def kernel(comm, pos_ref, vel_ref, rho_ref, mass_ref, kind_ref, rate_ref, acc_ref,
           ext, gext, raw, traw, feat_c, feat_d, feat_g, far, near, cfull, chalf, dfull, dhalf, sums, parts, gsums, off,
           send_sem, recv_sem, gsend_sem, grecv_sem):
    if comm:
        gx = lax.axis_index("gx")
        gy = lax.axis_index("gy")
        nx = lax.axis_size("gx")
        ny = lax.axis_size("gy")
    else:
        gx, gy, nx, ny = jnp.int32(1), jnp.int32(1), 16, 16

    def peer(i, j):
        return (lax.rem(gx + i + nx, nx), lax.rem(gy + j + ny, ny))

    if comm:
        barrier = pltpu.get_barrier_semaphore()
        for i, j in SIDES:
            pl.semaphore_signal(barrier, inc=1, device_id=peer(i, j), device_id_type=MESH)

    kind = kind_ref[...]
    rho = rho_ref[...]
    vol = jnp.where(kind > 0, mass_ref[...], 0.0) / rho * SCALE
    own = [pos_ref[0], pos_ref[1], pos_ref[2], vel_ref[0], vel_ref[1], vel_ref[2], rho - 1.0, vol]

    def spread_rows(buf, start, stride, value):
        for h in range(value.shape[0] // 8):
            buf[pl.ds(start + h * 8 * stride, 8, stride=stride), :] = value[h * 8:h * 8 + 8]

    def take_rows(buf, start, stride, count):
        return jnp.concatenate([buf[pl.ds(start + h * 8 * stride, 8, stride=stride), :] for h in range(count // 8)], axis=0)

    for ch in range(8):
        spread_rows(ext, ch, 8, own[ch])

    def swap(buf, rows, ssem, rsem):
        moves = []
        for i, j in SIDES:
            if j == 0:
                a = 1 if i > 0 else 0
                runs = [(2 * a, 4 + 2 * (1 - a), 2)]
            elif i == 0:
                b = 1 if j > 0 else 0
                runs = [(2 * a + b, 8 + 2 * (1 - b) + a, 1) for a in range(2)]
            else:
                a, b = (1 if i > 0 else 0), (1 if j > 0 else 0)
                runs = [(2 * a + b, 12 + 2 * (1 - a) + 1 - b, 1)]
            for src, dst, count in runs:
                n = len(moves)
                moves.append(pltpu.make_async_remote_copy(
                    src_ref=buf.at[pl.ds(src * rows, count * rows)],
                    dst_ref=buf.at[pl.ds(dst * rows, count * rows)],
                    send_sem=ssem.at[n], recv_sem=rsem.at[n],
                    device_id=peer(i, j), device_id_type=MESH))
        return moves

    ox = ((gx * 2 + 1) * 2).astype(F32)
    oy = ((gy * 2 + 1) * 2).astype(F32)

    xt = [own[0] - ox, own[1] - oy, own[2] - 4.0]
    for k, value in enumerate(distance_rows(xt, False)):
        spread_rows(traw, k, 24, value)
    for t in range(8):
        p = t % 2
        both = jnp.concatenate([traw[(2 * t + h) * 24:(2 * t + h + 1) * 24, :] for h in range(2)], axis=1)
        both = jnp.concatenate([both, jnp.zeros((8, 256), F32)], axis=0).astype(BF16)
        blocks = [(BOTH[p][0], both), (BOTH[p][1], both), (ONE[p], both[:, LANE[p]:LANE[p] + 128])]
        near[t] = jnp.concatenate(
            [jnp.concatenate([b if ly == at else jnp.zeros_like(b) for ly in range(4)], axis=0) for at, b in blocks], axis=1)

    eye = (lax.broadcasted_iota(jnp.int32, (128, 128), 0) == lax.broadcasted_iota(jnp.int32, (128, 128), 1))
    eye16 = jnp.where(eye, 1.0, 0.0).astype(BF16)
    off[...] = jnp.where(eye, 0.0, 1.0)

    def features(first, count, inside):
        def chan(ch):
            return take_rows(ext, first * 8 + ch, 8, count)

        x = [chan(0) - ox, chan(1) - oy, chan(2) - 4.0]
        v = [chan(3 + d) for d in range(3)]
        r = chan(6)
        w = chan(7)
        if inside is not None:
            w = jnp.where(inside, w, 0.0)
        pr = power7(r + 1.0)
        vx = v[0] * x[0] + v[1] * x[1] + v[2] * x[2]
        wx = [w * x[d] for d in range(3)]
        wxx = [wx[a] * x[b] for a in range(3) for b in range(a, 3)]
        wv = [w * v[d] for d in range(3)]
        wr = w * r
        wp = w * pr
        zero = jnp.zeros_like(w)
        rows = [w] + wx + wxx + [wr] + [wr * x[d] for d in range(3)] + wv + [w * vx] + [wp] + [wp * x[d] for d in range(3)]
        rows += [zero, zero]
        e, f = pieces(w), pieces(wr)
        rows += wv + wx + wxx + [wv[a] * x[b] for a in range(3) for b in range(3)] + [w * vx * x[d] for d in range(3)]
        rows += [e[0], f[0], e[1], f[1], e[2], f[2], zero, zero]
        rows += distance_rows(x, True)
        for f, value in enumerate(rows):
            spread_rows(raw, first * RAW + f, RAW, value)

    def column(c):
        dist = []
        for layer in range(4):
            cell = c * 4 + layer
            got = raw[pl.ds(pl.multiple_of(cell * RAW, 8), RAW), :]
            feat_c[cell] = jnp.concatenate(list(pieces(got[0:24])) + [jnp.zeros((8, 128), F32)], axis=0).astype(BF16)
            feat_d[cell] = jnp.concatenate(list(pieces(got[24:48])) + [got[48:56]], axis=0).astype(BF16)
            dist += [got[56:80], jnp.zeros((8, 128), F32)]
        dist = jnp.concatenate(dist, axis=0).astype(BF16)
        far[c] = lax.dot_general(eye16, dist, (((1,), (1,)), ((), ())), preferred_element_type=F32).astype(BF16)

    def two(x):
        hi = x.astype(BF16)
        lo = (x - hi.astype(F32)).astype(BF16)
        return jnp.concatenate([hi, lo], axis=0)

    def weigh(tc, p, col, full_c, half_c, full_d, half_d, self_col):
        gap = jnp.dot(far[col], near[tc * 2 + p], preferred_element_type=F32)
        for k in range(3):
            d2 = jnp.maximum(gap[:, 256 * k:min(256 * k + 256, 640)], TINY)
            wedge = jnp.maximum(1.0 - d2 * lax.rsqrt(d2), 0.0)
            c = wedge * wedge * wedge
            d = c * pl.reciprocal(d2 + SOFT4, approx=True)
            if self_col and k < 2:
                halves = [d[:, 0:128], d[:, 128:256]]
                halves[k] = halves[k] * off[...]
                d = jnp.concatenate(halves, axis=1)
            if k < 2:
                full_c[k * 256:k * 256 + 256] = two(c)
                full_d[k * 256:k * 256 + 256] = two(d)
            else:
                half_c[...] = two(c)
                half_d[...] = two(d)

    def total(feat, rows, p, cols, full, half):
        lf, lh = [], []
        for c in cols:
            for ly in BOTH[p]:
                lf += [feat[c * 4 + ly]] * 2
            lh += [feat[c * 4 + ONE[p]]] * 2
        n = len(cols)
        f = jnp.dot(jnp.concatenate(lf, axis=1), full.reshape(n * 512, 256), preferred_element_type=F32)
        h = jnp.dot(jnp.concatenate(lh, axis=1), half.reshape(n * 256, 128), preferred_element_type=F32)
        return (f[:, 0:128], f[:, 128:256] + h) if p == 0 else (f[:, 0:128] + h, f[:, 128:256])

    def mates(tc):
        return [lax.rem(tc + k, 4) for k in range(4)]

    def halo(tc):
        a, b = tc // 2, lax.rem(tc, 2)
        return [4 + 2 * a, 5 + 2 * a, 8 + 2 * b, 9 + 2 * b, 12 + tc]

    def fold(s):
        return s[0:24] + s[24:48] + s[48:72]

    features(0, 16, None)
    for c in range(4):
        column(c)

    def own_pairs(tc):
        for p in range(2):
            cols = mates(tc)
            for k in range(4):
                weigh(tc, p, cols[k], cfull.at[p, tc, k], chalf.at[p, tc, k], dfull.at[p, tc, k], dhalf.at[p, tc, k], k == 0)
            for which, (feat, full, half) in enumerate(((feat_c, cfull, chalf), (feat_d, dfull, dhalf))):
                got = total(feat, 80, p, cols, full[p, tc, 0:4], half[p, tc, 0:4])
                for h in range(2):
                    sums[tc * 2 + p, h, which * 80:which * 80 + 80] = got[h]

    pl.loop(0, CUT)(own_pairs)
    if comm:
        pl.semaphore_wait(barrier, 8)
        moves = swap(ext, 32, send_sem, recv_sem)
        for c in moves:
            c.start()
    pl.loop(CUT, 4)(own_pairs)
    if comm:
        for c in moves:
            c.wait()

    cell = lax.broadcasted_iota(jnp.int32, (48, 128), 0) // 4 + 4
    group = cell // 2
    below_a = (group == 2) | (cell == 12) | (cell == 13)
    above_a = (group == 3) | (cell == 14) | (cell == 15)
    below_b = (group == 4) | (cell == 12) | (cell == 14)
    above_b = (group == 5) | (cell == 13) | (cell == 15)
    outside = (below_a & (gx == 0)) | (above_a & (gx == nx - 1)) | (below_b & (gy == 0)) | (above_b & (gy == ny - 1))
    features(16, 48, jnp.logical_not(outside))

    @pl.loop(0, 3)
    def _(n):
        for k in range(4):
            column(4 + n * 4 + k)

    @pl.loop(0, 4)
    def _(tc):
        for p in range(2):
            cols = halo(tc)
            for k in range(5):
                weigh(tc, p, cols[k], cfull.at[p, tc, 4 + k], chalf.at[p, tc, 4 + k], dfull.at[p, tc, k],
                      dhalf.at[p, tc, k], False)
            got = total(feat_c, 80, p, cols, cfull[p, tc, 4:9], chalf[p, tc, 4:9])
            for h in range(2):
                base = pl.multiple_of((tc * 4 + p * 2 + h) * 56, 8)
                parts[pl.ds(base, 24), :] = fold(sums[tc * 2 + p, h, 0:80] + got[h])

    def part(f, stride=56):
        return take_rows(parts, f, stride, 16)

    def dot3(a, b):
        return a[0] * b[0] + a[1] * b[1] + a[2] * b[2]

    pc = [part(f) for f in range(22)]
    s0, s1, sr, srx, sv, svx, sp, spx = pc[0], pc[1:4], pc[10], pc[11:14], pc[14:17], pc[17], pc[18], pc[19:22]
    pair = {}
    n = 0
    for a in range(3):
        for b in range(a, 3):
            pair[a, b] = pair[b, a] = n
            n += 1
    mom = {}
    for a in range(3):
        for b in range(a, 3):
            m = -(pc[4 + pair[a, b]] - xt[a] * s1[b] - xt[b] * (s1[a] - xt[a] * s0))
            mom[a, b] = m + FLOOR if a == b else m
    rt = own[6]
    back = [s0 * xt[a] - s1[a] for a in range(3)]
    slope = [(sr * xt[a] - srx[a]) - rt * back[a] for a in range(3)]
    m00, m01, m02, m11, m12, m22 = mom[0, 0], mom[0, 1], mom[0, 2], mom[1, 1], mom[1, 2], mom[2, 2]
    c00 = m11 * m22 - m12 * m12
    c01 = m02 * m12 - m01 * m22
    c02 = m01 * m12 - m02 * m11
    c11 = m00 * m22 - m02 * m02
    c12 = m01 * m02 - m00 * m12
    c22 = m00 * m11 - m01 * m01
    det = m00 * c00 + m01 * c01 + m02 * c02
    grad = [(c00 * slope[0] + c01 * slope[1] + c02 * slope[2]) / det,
            (c01 * slope[0] + c11 * slope[1] + c12 * slope[2]) / det,
            (c02 * slope[0] + c12 * slope[1] + c22 * slope[2]) / det]

    for d in range(3):
        spread_rows(gext, d, 4, grad[d])
    if comm:
        moves = swap(gext, 16, gsend_sem, grecv_sem)
        for c in moves:
            c.start()

    @pl.loop(0, 4)
    def _(tc):
        for p in range(2):
            got = total(feat_d, 80, p, halo(tc), dfull[p, tc, 0:5], dhalf[p, tc, 0:5])
            for h in range(2):
                s = sums[tc * 2 + p, h, 80:160] + got[h]
                base = pl.multiple_of((tc * 4 + p * 2 + h) * 56, 8)
                parts[pl.ds(base + 24, 24), :] = fold(s)
                parts[pl.ds(base + 48, 8), :] = s[72:80]

    def slopes(first, count, inside):
        x = [take_rows(ext, first * 8 + d, 8, count) - o for d, o in enumerate((ox, oy, 4.0))]
        w = take_rows(ext, first * 8 + 7, 8, count)
        if inside is not None:
            w = jnp.where(inside, w, 0.0)
        g = [take_rows(gext, first * 4 + d, 4, count) for d in range(3)]
        rows = [pieces(w * g[d]) for d in range(3)] + [pieces(w * dot3(g, x))]
        for k in range(3):
            for f in range(4):
                spread_rows(raw, first * 16 + k * 4 + f, 16, rows[f][k])
        for f in range(12, 16):
            spread_rows(raw, first * 16 + f, 16, jnp.zeros_like(w))
        for n in range(first, first + count):
            feat_g[n] = raw[n * 16:n * 16 + 16, :].astype(BF16)

    slopes(0, 16, None)

    @pl.loop(0, 4)
    def _(tc):
        for p in range(2):
            got = total(feat_g, 16, p, mates(tc), cfull[p, tc, 0:4], chalf[p, tc, 0:4])
            for h in range(2):
                gsums[tc * 2 + p, h] = got[h]

    vt = own[3:6]
    pt = power7(rho)
    vtx = dot3(vt, xt)
    flow = dot3(sv, xt) - svx - vtx * s0 + dot3(vt, s1)
    pd = [part(24 + f) for f in range(30)]
    d0 = pd[24] + pd[26] + pd[28]
    dr = pd[25] + pd[27] + pd[29]
    dv, d1, dxx, dvx, dvxx = pd[0:3], pd[3:6], pd[6:12], [pd[12:15], pd[15:18], pd[18:21]], pd[21:24]
    spread = -2.0 * ((sr - rt * s0) - SOFT4 * (dr - rt * d0))
    trace = dvx[0][0] + dvx[1][1] + dvx[2][2]
    head = dot3(dv, xt) - trace - vtx * d0 + dot3(vt, d1)
    push = []
    for b in range(3):
        tail = (xt[0] * dvx[0][b] + xt[1] * dvx[1][b] + xt[2] * dvx[2][b] - dvxx[b] - vtx * d1[b]
                + vt[0] * dxx[pair[0, b]] + vt[1] * dxx[pair[1, b]] + vt[2] * dxx[pair[2, b]])
        push.append(-(pt * back[b] + (sp * xt[b] - spx[b])) - (0.25 * ALPHA_SOUND) * (xt[b] * head - tail))
    moving = kind == 1
    for b in range(3):
        force = push[b] / rho - (GRAVITY if b == 2 else 0.0)
        acc_ref[b] = jnp.where(moving, force, 0.0)
    spread = spread - dot3(grad, back)

    if comm:
        for c in moves:
            c.wait()
    slopes(16, 48, jnp.logical_not(outside))

    @pl.loop(0, 4)
    def _(tc):
        for p in range(2):
            got = total(feat_g, 16, p, halo(tc), cfull[p, tc, 4:9], chalf[p, tc, 4:9])
            for h in range(2):
                base = pl.multiple_of((tc * 4 + p * 2 + h) * 16, 8)
                parts[pl.ds(base, 16), :] = gsums[tc * 2 + p, h] + got[h]

    q = [part(f, 16) for f in range(12)]
    q = [q[f] + q[f + 4] + q[f + 8] for f in range(4)]
    spread = spread - (dot3(q, xt) - q[3])
    rate = -rho * flow + DELTA_SOUND * spread
    rate_ref[...] = jnp.where(kind > 0, rate, 0.0)


def local(comm, positions, velocity, density, mass, kind):
    vmem = pl.BlockSpec(memory_space=pltpu.VMEM)
    dma = pltpu.SemaphoreType.DMA
    rate, acc = pl.pallas_call(
        functools.partial(kernel, comm),
        out_shape=(jax.ShapeDtypeStruct((16, 128), F32), jax.ShapeDtypeStruct((3, 16, 128), F32)),
        in_specs=[vmem] * 5,
        out_specs=(vmem, vmem),
        scratch_shapes=[
            pltpu.VMEM((512, 128), F32),
            pltpu.VMEM((256, 128), F32),
            pltpu.VMEM((64 * RAW, 128), F32),
            pltpu.VMEM((16 * 24, 128), F32),
            pltpu.VMEM((64, 80, 128), BF16),
            pltpu.VMEM((64, 80, 128), BF16),
            pltpu.VMEM((64, 16, 128), BF16),
            pltpu.VMEM((16, 128, 128), BF16),
            pltpu.VMEM((8, 128, 640), BF16),
            pltpu.VMEM((2, 4, 9, 512, 256), BF16),
            pltpu.VMEM((2, 4, 9, 256, 128), BF16),
            pltpu.VMEM((2, 4, 5, 512, 256), BF16),
            pltpu.VMEM((2, 4, 5, 256, 128), BF16),
            pltpu.VMEM((8, 2, 160, 128), F32),
            pltpu.VMEM((16 * 56, 128), F32),
            pltpu.VMEM((8, 2, 16, 128), F32),
            pltpu.VMEM((128, 128), F32),
            dma((10,)), dma((10,)), dma((10,)), dma((10,)),
        ],
        compiler_params=pltpu.CompilerParams(
            vmem_limit_bytes=56 * 1024 * 1024,
            **(dict(collective_id=0, has_side_effects=True) if comm else {})),
        cost_estimate=pl.CostEstimate(flops=2 * 10**9, bytes_accessed=10**6, transcendentals=10**7),
    )(positions.reshape(3, 16, 128), velocity.reshape(3, 16, 128), density.reshape(16, 128),
      mass.reshape(16, 128), kind.reshape(16, 128))
    return rate.reshape(2, 2, 4, 128), acc.reshape(3, 2, 2, 4, 128)


def solution(mesh):
    in_specs = (
        P(None, "gx", "gy", None, None),
        P(None, "gx", "gy", None, None),
        P("gx", "gy", None, None),
        P("gx", "gy", None, None),
        P("gx", "gy", None, None),
    )
    out_specs = (P("gx", "gy", None, None), P(None, "gx", "gy", None, None))
    return jax.shard_map(functools.partial(local, True), mesh=mesh, in_specs=in_specs, out_specs=out_specs,
                         check_vma=False)
```

```python
import functools
import math

import jax
import jax.numpy as jnp
from jax import lax
from jax.experimental import pallas as pl
from jax.experimental.pallas import tpu as pltpu
from jax.sharding import PartitionSpec as P

MESH = pl.DeviceIdType.MESH
KERNEL_NORM = 21.0 / (16.0 * math.pi)
SCALE = -5.0 * KERNEL_NORM
STIFF = 9.0 / 7.0
DELTA_SOUND = 0.3
ALPHA_SOUND = 0.3
FLOOR = 0.25
GRAVITY = 1.0
SOFT4 = 0.0025

F32 = jnp.float32
BF16 = jnp.bfloat16
RAW = 80
SIDES = [(i, j) for i in (-1, 0, 1) for j in (-1, 0, 1) if (i, j) != (0, 0)]
TINY = 1e-12
BOTH = {0: (0, 1), 1: (2, 3)}
ONE = {0: 2, 1: 1}
LANE = {0: 128, 1: 0}
CUT = 2
WIDTH = 256
ROWS = 128


def pieces(x):
    a = x.astype(BF16).astype(F32)
    r = x - a
    b = r.astype(BF16).astype(F32)
    return a, b, r - b


def power7(r):
    r2 = r * r
    r4 = r2 * r2
    return STIFF * (r4 * r2 * r - 1.0)


def distance_rows(xs, source):
    half = [0.5 * x for x in xs]
    cut = [pieces(h) for h in half]
    norm = pieces(half[0] * half[0] + half[1] * half[1] + half[2] * half[2])
    one = jnp.ones_like(half[0])
    rows = []
    for i in range(3):
        for j in range(3 - i):
            for d in range(3):
                rows.append(-2.0 * cut[d][i] if source else cut[d][j])
    rows += list(norm) + [one] * 3 if source else [one] * 3 + list(norm)
    return rows


def kernel(comm, pos_ref, vel_ref, rho_ref, mass_ref, kind_ref, rate_ref, acc_ref,
           ext, gext, raw, traw, feat_c, feat_d, feat_g, far, near, cfull, chalf, dfull, dhalf, sums, parts, gsums, off,
           send_sem, recv_sem, gsend_sem, grecv_sem):
    if comm:
        gx = lax.axis_index("gx")
        gy = lax.axis_index("gy")
        nx = lax.axis_size("gx")
        ny = lax.axis_size("gy")
    else:
        gx, gy, nx, ny = jnp.int32(1), jnp.int32(1), 16, 16

    def peer(i, j):
        return (lax.rem(gx + i + nx, nx), lax.rem(gy + j + ny, ny))

    if comm:
        barrier = pltpu.get_barrier_semaphore()
        for i, j in SIDES:
            pl.semaphore_signal(barrier, inc=1, device_id=peer(i, j), device_id_type=MESH)

    kind = kind_ref[...]
    rho = rho_ref[...]
    vol = jnp.where(kind > 0, mass_ref[...], 0.0) / rho * SCALE
    own = [pos_ref[0], pos_ref[1], pos_ref[2], vel_ref[0], vel_ref[1], vel_ref[2], rho - 1.0, vol]

    def spread_rows(buf, start, stride, value):
        for h in range(value.shape[0] // 8):
            buf[pl.ds(start + h * 8 * stride, 8, stride=stride), :] = value[h * 8:h * 8 + 8]

    def take_rows(buf, start, stride, count):
        return jnp.concatenate([buf[pl.ds(start + h * 8 * stride, 8, stride=stride), :] for h in range(count // 8)], axis=0)

    for ch in range(8):
        spread_rows(ext, ch, 8, own[ch])

    def swap(buf, rows, ssem, rsem):
        moves = []
        for i, j in SIDES:
            if j == 0:
                a = 1 if i > 0 else 0
                runs = [(2 * a, 4 + 2 * (1 - a), 2)]
            elif i == 0:
                b = 1 if j > 0 else 0
                runs = [(2 * a + b, 8 + 2 * (1 - b) + a, 1) for a in range(2)]
            else:
                a, b = (1 if i > 0 else 0), (1 if j > 0 else 0)
                runs = [(2 * a + b, 12 + 2 * (1 - a) + 1 - b, 1)]
            for src, dst, count in runs:
                n = len(moves)
                moves.append(pltpu.make_async_remote_copy(
                    src_ref=buf.at[pl.ds(src * rows, count * rows)],
                    dst_ref=buf.at[pl.ds(dst * rows, count * rows)],
                    send_sem=ssem.at[n], recv_sem=rsem.at[n],
                    device_id=peer(i, j), device_id_type=MESH))
        return moves

    ox = ((gx * 2 + 1) * 2).astype(F32)
    oy = ((gy * 2 + 1) * 2).astype(F32)

    xt = [own[0] - ox, own[1] - oy, own[2] - 4.0]
    for k, value in enumerate(distance_rows(xt, False)):
        spread_rows(traw, k, 24, value)
    for t in range(8):
        p = t % 2
        both = jnp.concatenate([traw[(2 * t + h) * 24:(2 * t + h + 1) * 24, :] for h in range(2)], axis=1)
        both = jnp.concatenate([both, jnp.zeros((8, 256), F32)], axis=0).astype(BF16)
        blocks = [(BOTH[p][0], both), (BOTH[p][1], both), (ONE[p], both[:, LANE[p]:LANE[p] + 128])]
        near[t] = jnp.concatenate(
            [jnp.concatenate([b if ly == at else jnp.zeros_like(b) for ly in range(4)], axis=0) for at, b in blocks], axis=1)

    eye = (lax.broadcasted_iota(jnp.int32, (128, 128), 0) == lax.broadcasted_iota(jnp.int32, (128, 128), 1))
    eye16 = jnp.where(eye, 1.0, 0.0).astype(BF16)
    off[...] = jnp.where(eye, 0.0, 1.0)

    def features(first, count, inside):
        def chan(ch):
            return take_rows(ext, first * 8 + ch, 8, count)

        x = [chan(0) - ox, chan(1) - oy, chan(2) - 4.0]
        v = [chan(3 + d) for d in range(3)]
        r = chan(6)
        w = chan(7)
        if inside is not None:
            w = jnp.where(inside, w, 0.0)
        pr = power7(r + 1.0)
        vx = v[0] * x[0] + v[1] * x[1] + v[2] * x[2]
        wx = [w * x[d] for d in range(3)]
        wxx = [wx[a] * x[b] for a in range(3) for b in range(a, 3)]
        wv = [w * v[d] for d in range(3)]
        wr = w * r
        wp = w * pr
        zero = jnp.zeros_like(w)
        rows = [w] + wx + wxx + [wr] + [wr * x[d] for d in range(3)] + wv + [w * vx] + [wp] + [wp * x[d] for d in range(3)]
        rows += [zero, zero]
        e, f = pieces(w), pieces(wr)
        rows += wv + wx + wxx + [wv[a] * x[b] for a in range(3) for b in range(3)] + [w * vx * x[d] for d in range(3)]
        rows += [e[0], f[0], e[1], f[1], e[2], f[2], zero, zero]
        rows += distance_rows(x, True)
        for f, value in enumerate(rows):
            spread_rows(raw, first * RAW + f, RAW, value)

    def column(c):
        dist = []
        for layer in range(4):
            cell = c * 4 + layer
            got = raw[pl.ds(pl.multiple_of(cell * RAW, 8), RAW), :]
            feat_c[cell] = jnp.concatenate(list(pieces(got[0:24])) + [jnp.zeros((8, 128), F32)], axis=0).astype(BF16)
            feat_d[cell] = jnp.concatenate(list(pieces(got[24:48])) + [got[48:56]], axis=0).astype(BF16)
            dist += [got[56:80], jnp.zeros((8, 128), F32)]
        dist = jnp.concatenate(dist, axis=0).astype(BF16)
        far[c] = lax.dot_general(eye16, dist, (((1,), (1,)), ((), ())), preferred_element_type=F32).astype(BF16)

    def two(x):
        hi = x.astype(BF16)
        lo = (x - hi.astype(F32)).astype(BF16)
        return hi, lo

    def weigh(tc, p, col, full_c, half_c, full_d, half_d, self_col):
        lhs = far[col]
        for at in range(0, 640, WIDTH):
          for r in range(0, 128, ROWS):
            gap = jnp.dot(lhs[r:r + ROWS], near[tc * 2 + p, :, at:min(at + WIDTH, 640)], preferred_element_type=F32)
            d2 = jnp.maximum(gap, TINY)
            wedge = jnp.maximum(1.0 - d2 * lax.rsqrt(d2), 0.0)
            c = wedge * wedge * wedge
            d = c * pl.reciprocal(d2 + SOFT4, approx=True)
            k = at // 256
            if self_col and k < 2 and at <= 384 * k < at + WIDTH:
                parts_d = [d[:, j:j + 128] for j in range(0, d.shape[1], 128)]
                parts_d[(384 * k - at) // 128] *= off[r:r + ROWS]
                d = jnp.concatenate(parts_d, axis=1)
            lane = at % 256
            for (hi, lo), full, half in ((two(c), full_c, half_c), (two(d), full_d, half_d)):
                out = full.at[k * 256:k * 256 + 256, lane:lane + gap.shape[1]] if k < 2 else half
                out[r:r + ROWS] = hi
                out[128 + r:128 + r + ROWS] = lo

    def total(feat, rows, p, cols, full, half):
        lf, lh = [], []
        for c in cols:
            for ly in BOTH[p]:
                lf += [feat[c * 4 + ly]] * 2
            lh += [feat[c * 4 + ONE[p]]] * 2
        n = len(cols)
        f = jnp.dot(jnp.concatenate(lf, axis=1), full.reshape(n * 512, 256), preferred_element_type=F32)
        h = jnp.dot(jnp.concatenate(lh, axis=1), half.reshape(n * 256, 128), preferred_element_type=F32)
        return (f[:, 0:128], f[:, 128:256] + h) if p == 0 else (f[:, 0:128] + h, f[:, 128:256])

    def mates(tc):
        return [(tc + k) % 4 for k in range(4)]

    def halo(tc):
        a, b = tc // 2, tc % 2
        return [4 + 2 * a, 5 + 2 * a, 8 + 2 * b, 9 + 2 * b, 12 + tc]

    def fold(s):
        return s[0:24] + s[24:48] + s[48:72]

    features(0, 16, None)
    for c in range(4):
        column(c)

    def own_weights(tc):
        for p in range(2):
            cols = mates(tc)
            for k in range(4):
                weigh(tc, p, cols[k], cfull.at[p, tc, k], chalf.at[p, tc, k], dfull.at[p, tc, k], dhalf.at[p, tc, k], k == 0)

    def own_sums(tc):
        for p in range(2):
            for which, (feat, full, half) in enumerate(((feat_c, cfull, chalf), (feat_d, dfull, dhalf))):
                got = total(feat, 80, p, mates(tc), full[p, tc, 0:4], half[p, tc, 0:4])
                for h in range(2):
                    sums[tc * 2 + p, h, which * 80:which * 80 + 80] = got[h]

    for tc in range(CUT):
        own_weights(tc)
    if comm:
        pl.semaphore_wait(barrier, 8)
        moves = swap(ext, 32, send_sem, recv_sem)
        for c in moves:
            c.start()
    for tc in range(CUT, 4):
        own_weights(tc)
    for tc in range(4):
        own_sums(tc)
    if comm:
        for c in moves:
            c.wait()

    cell = lax.broadcasted_iota(jnp.int32, (48, 128), 0) // 4 + 4
    group = cell // 2
    below_a = (group == 2) | (cell == 12) | (cell == 13)
    above_a = (group == 3) | (cell == 14) | (cell == 15)
    below_b = (group == 4) | (cell == 12) | (cell == 14)
    above_b = (group == 5) | (cell == 13) | (cell == 15)
    outside = (below_a & (gx == 0)) | (above_a & (gx == nx - 1)) | (below_b & (gy == 0)) | (above_b & (gy == ny - 1))
    features(16, 48, jnp.logical_not(outside))

    for c in range(4, 16):
        column(c)
    for tc in range(4):
        for p in range(2):
            cols = halo(tc)
            for k in range(5):
                weigh(tc, p, cols[k], cfull.at[p, tc, 4 + k], chalf.at[p, tc, 4 + k], dfull.at[p, tc, k],
                      dhalf.at[p, tc, k], False)
    for tc in range(4):
        for p in range(2):
            got = total(feat_c, 80, p, halo(tc), cfull[p, tc, 4:9], chalf[p, tc, 4:9])
            for h in range(2):
                base = (tc * 4 + p * 2 + h) * 56
                parts[base:base + 24, :] = fold(sums[tc * 2 + p, h, 0:80] + got[h])

    def part(f, stride=56):
        return take_rows(parts, f, stride, 16)

    def dot3(a, b):
        return a[0] * b[0] + a[1] * b[1] + a[2] * b[2]

    pc = [part(f) for f in range(22)]
    s0, s1, sr, srx, sv, svx, sp, spx = pc[0], pc[1:4], pc[10], pc[11:14], pc[14:17], pc[17], pc[18], pc[19:22]
    pair = {}
    n = 0
    for a in range(3):
        for b in range(a, 3):
            pair[a, b] = pair[b, a] = n
            n += 1
    mom = {}
    for a in range(3):
        for b in range(a, 3):
            m = -(pc[4 + pair[a, b]] - xt[a] * s1[b] - xt[b] * (s1[a] - xt[a] * s0))
            mom[a, b] = m + FLOOR if a == b else m
    rt = own[6]
    back = [s0 * xt[a] - s1[a] for a in range(3)]
    slope = [(sr * xt[a] - srx[a]) - rt * back[a] for a in range(3)]
    m00, m01, m02, m11, m12, m22 = mom[0, 0], mom[0, 1], mom[0, 2], mom[1, 1], mom[1, 2], mom[2, 2]
    c00 = m11 * m22 - m12 * m12
    c01 = m02 * m12 - m01 * m22
    c02 = m01 * m12 - m02 * m11
    c11 = m00 * m22 - m02 * m02
    c12 = m01 * m02 - m00 * m12
    c22 = m00 * m11 - m01 * m01
    det = m00 * c00 + m01 * c01 + m02 * c02
    grad = [(c00 * slope[0] + c01 * slope[1] + c02 * slope[2]) / det,
            (c01 * slope[0] + c11 * slope[1] + c12 * slope[2]) / det,
            (c02 * slope[0] + c12 * slope[1] + c22 * slope[2]) / det]

    for d in range(3):
        spread_rows(gext, d, 4, grad[d])
    if comm:
        moves = swap(gext, 16, gsend_sem, grecv_sem)
        for c in moves:
            c.start()

    for tc in range(4):
        for p in range(2):
            got = total(feat_d, 80, p, halo(tc), dfull[p, tc, 0:5], dhalf[p, tc, 0:5])
            for h in range(2):
                s = sums[tc * 2 + p, h, 80:160] + got[h]
                base = (tc * 4 + p * 2 + h) * 56
                parts[pl.ds(base + 24, 24), :] = fold(s)
                parts[pl.ds(base + 48, 8), :] = s[72:80]

    def slopes(first, count, inside):
        x = [take_rows(ext, first * 8 + d, 8, count) - o for d, o in enumerate((ox, oy, 4.0))]
        w = take_rows(ext, first * 8 + 7, 8, count)
        if inside is not None:
            w = jnp.where(inside, w, 0.0)
        g = [take_rows(gext, first * 4 + d, 4, count) for d in range(3)]
        rows = [pieces(w * g[d]) for d in range(3)] + [pieces(w * dot3(g, x))]
        for k in range(3):
            for f in range(4):
                spread_rows(raw, first * 16 + k * 4 + f, 16, rows[f][k])
        for f in range(12, 16):
            spread_rows(raw, first * 16 + f, 16, jnp.zeros_like(w))
        for n in range(first, first + count):
            feat_g[n] = raw[n * 16:n * 16 + 16, :].astype(BF16)

    slopes(0, 16, None)

    for tc in range(4):
        for p in range(2):
            got = total(feat_g, 16, p, mates(tc), cfull[p, tc, 0:4], chalf[p, tc, 0:4])
            for h in range(2):
                gsums[tc * 2 + p, h] = got[h]

    vt = own[3:6]
    pt = power7(rho)
    vtx = dot3(vt, xt)
    flow = dot3(sv, xt) - svx - vtx * s0 + dot3(vt, s1)
    pd = [part(24 + f) for f in range(30)]
    d0 = pd[24] + pd[26] + pd[28]
    dr = pd[25] + pd[27] + pd[29]
    dv, d1, dxx, dvx, dvxx = pd[0:3], pd[3:6], pd[6:12], [pd[12:15], pd[15:18], pd[18:21]], pd[21:24]
    spread = -2.0 * ((sr - rt * s0) - SOFT4 * (dr - rt * d0))
    trace = dvx[0][0] + dvx[1][1] + dvx[2][2]
    head = dot3(dv, xt) - trace - vtx * d0 + dot3(vt, d1)
    push = []
    for b in range(3):
        tail = (xt[0] * dvx[0][b] + xt[1] * dvx[1][b] + xt[2] * dvx[2][b] - dvxx[b] - vtx * d1[b]
                + vt[0] * dxx[pair[0, b]] + vt[1] * dxx[pair[1, b]] + vt[2] * dxx[pair[2, b]])
        push.append(-(pt * back[b] + (sp * xt[b] - spx[b])) - (0.25 * ALPHA_SOUND) * (xt[b] * head - tail))
    moving = kind == 1
    for b in range(3):
        force = push[b] / rho - (GRAVITY if b == 2 else 0.0)
        acc_ref[b] = jnp.where(moving, force, 0.0)
    spread = spread - dot3(grad, back)

    if comm:
        for c in moves:
            c.wait()
    slopes(16, 48, jnp.logical_not(outside))

    for tc in range(4):
        for p in range(2):
            got = total(feat_g, 16, p, halo(tc), cfull[p, tc, 4:9], chalf[p, tc, 4:9])
            for h in range(2):
                base = (tc * 4 + p * 2 + h) * 16
                parts[pl.ds(base, 16), :] = gsums[tc * 2 + p, h] + got[h]

    q = [part(f, 16) for f in range(12)]
    q = [q[f] + q[f + 4] + q[f + 8] for f in range(4)]
    spread = spread - (dot3(q, xt) - q[3])
    rate = -rho * flow + DELTA_SOUND * spread
    rate_ref[...] = jnp.where(kind > 0, rate, 0.0)


def last(a_ref, b_ref, rate_ref, acc_ref):
    rate_ref[...] = a_ref[...]
    acc_ref[...] = b_ref[...]


def finish(rate, acc):
    vmem = pl.BlockSpec(memory_space=pltpu.VMEM)
    return pl.pallas_call(
        last,
        out_shape=(jax.ShapeDtypeStruct((16, 128), F32), jax.ShapeDtypeStruct((3, 16, 128), F32)),
        in_specs=[vmem, vmem],
        out_specs=(vmem, vmem),
    )(rate, acc)


def local(comm, positions, velocity, density, mass, kind):
    vmem = pl.BlockSpec(memory_space=pltpu.VMEM)
    dma = pltpu.SemaphoreType.DMA
    rate, acc = pl.pallas_call(
        functools.partial(kernel, comm),
        out_shape=(jax.ShapeDtypeStruct((16, 128), F32), jax.ShapeDtypeStruct((3, 16, 128), F32)),
        in_specs=[vmem] * 5,
        out_specs=(vmem, vmem),
        scratch_shapes=[
            pltpu.VMEM((512, 128), F32),
            pltpu.VMEM((256, 128), F32),
            pltpu.VMEM((64 * RAW, 128), F32),
            pltpu.VMEM((16 * 24, 128), F32),
            pltpu.VMEM((64, 80, 128), BF16),
            pltpu.VMEM((64, 80, 128), BF16),
            pltpu.VMEM((64, 16, 128), BF16),
            pltpu.VMEM((16, 128, 128), BF16),
            pltpu.VMEM((8, 128, 640), BF16),
            pltpu.VMEM((2, 4, 9, 512, 256), BF16),
            pltpu.VMEM((2, 4, 9, 256, 128), BF16),
            pltpu.VMEM((2, 4, 5, 512, 256), BF16),
            pltpu.VMEM((2, 4, 5, 256, 128), BF16),
            pltpu.VMEM((8, 2, 160, 128), F32),
            pltpu.VMEM((16 * 56, 128), F32),
            pltpu.VMEM((8, 2, 16, 128), F32),
            pltpu.VMEM((128, 128), F32),
            dma((10,)), dma((10,)), dma((10,)), dma((10,)),
        ],
        compiler_params=pltpu.CompilerParams(
            vmem_limit_bytes=56 * 1024 * 1024,
            **(dict(collective_id=0, has_side_effects=True) if comm else {})),
        cost_estimate=pl.CostEstimate(flops=2 * 10**9, bytes_accessed=10**6, transcendentals=10**7),
    )(positions.reshape(3, 16, 128), velocity.reshape(3, 16, 128), density.reshape(16, 128),
      mass.reshape(16, 128), kind.reshape(16, 128))
    rate, acc = finish(rate, acc)
    return rate.reshape(2, 2, 4, 128), acc.reshape(3, 2, 2, 4, 128)


def solution(mesh):
    in_specs = (
        P(None, "gx", "gy", None, None),
        P(None, "gx", "gy", None, None),
        P("gx", "gy", None, None),
        P("gx", "gy", None, None),
        P("gx", "gy", None, None),
    )
    out_specs = (P("gx", "gy", None, None), P(None, "gx", "gy", None, None))
    return jax.shard_map(functools.partial(local, True), mesh=mesh, in_specs=in_specs, out_specs=out_specs,
                         check_vma=False)
```

```python
import functools
import math

import jax
import jax.numpy as jnp
from jax import lax
from jax.experimental import pallas as pl
from jax.experimental.pallas import tpu as pltpu
from jax.sharding import PartitionSpec as P

MESH = pl.DeviceIdType.MESH
KERNEL_NORM = 21.0 / (16.0 * math.pi)
SCALE = -5.0 * KERNEL_NORM
STIFF = 9.0 / 7.0
DELTA_SOUND = 0.3
ALPHA_SOUND = 0.3
FLOOR = 0.25
GRAVITY = 1.0
SOFT4 = 0.0025

F32 = jnp.float32
BF16 = jnp.bfloat16
RAW = 48
RAW_D = 32
SIDES = [(i, j) for i in (-1, 0, 1) for j in (-1, 0, 1) if (i, j) != (0, 0)]
TINY = 1e-12
BOTH = {0: (0, 1), 1: (2, 3)}
ONE = {0: 2, 1: 1}
LANE = {0: 128, 1: 0}
CUT = 2
WIDTH = 256
ROWS = 128


def pieces(x):
    a = x.astype(BF16).astype(F32)
    r = x - a
    b = r.astype(BF16).astype(F32)
    return a, b, r - b


def power7(r):
    r2 = r * r
    r4 = r2 * r2
    return STIFF * (r4 * r2 * r - 1.0)


def distance_rows(xs, source):
    half = [0.5 * x for x in xs]
    cut = [pieces(h) for h in half]
    norm = pieces(half[0] * half[0] + half[1] * half[1] + half[2] * half[2])
    one = jnp.ones_like(half[0])
    rows = []
    for i in range(3):
        for j in range(3 - i):
            for d in range(3):
                rows.append(-2.0 * cut[d][i] if source else cut[d][j])
    rows += list(norm) + [one] * 3 if source else [one] * 3 + list(norm)
    return rows


def kernel(comm, pos_ref, vel_ref, rho_ref, mass_ref, kind_ref, rate_ref, acc_ref,
           ext, gext, raw, traw, feat_c, feat_d, feat_g, far, near, cfull, chalf, dfull, dhalf, sums, parts, gsums, off,
           send_sem, recv_sem, gsend_sem, grecv_sem):
    if comm:
        gx = lax.axis_index("gx")
        gy = lax.axis_index("gy")
        nx = lax.axis_size("gx")
        ny = lax.axis_size("gy")
    else:
        gx, gy, nx, ny = jnp.int32(1), jnp.int32(1), 16, 16

    def peer(i, j):
        return (lax.rem(gx + i + nx, nx), lax.rem(gy + j + ny, ny))

    if comm:
        barrier = pltpu.get_barrier_semaphore()
        for i, j in SIDES:
            pl.semaphore_signal(barrier, inc=1, device_id=peer(i, j), device_id_type=MESH)

    kind = kind_ref[...]
    rho = rho_ref[...]
    vol = jnp.where(kind > 0, mass_ref[...], 0.0) / rho * SCALE
    own = [pos_ref[0], pos_ref[1], pos_ref[2], vel_ref[0], vel_ref[1], vel_ref[2], rho - 1.0, vol]

    def spread_rows(buf, start, stride, value):
        for h in range(value.shape[0] // 8):
            buf[pl.ds(start + h * 8 * stride, 8, stride=stride), :] = value[h * 8:h * 8 + 8]

    def take_rows(buf, start, stride, count):
        return jnp.concatenate([buf[pl.ds(start + h * 8 * stride, 8, stride=stride), :] for h in range(count // 8)], axis=0)

    for ch in range(8):
        spread_rows(ext, ch, 8, own[ch])

    def swap(buf, rows, ssem, rsem):
        moves = []
        kinds = ([], [], [])
        for i, j in SIDES:
            if j == 0:
                a = 1 if i > 0 else 0
                runs = [(2 * a, 4 + 2 * (1 - a), 2)]
            elif i == 0:
                b = 1 if j > 0 else 0
                runs = [(2 * a + b, 8 + 2 * (1 - b) + a, 1) for a in range(2)]
            else:
                a, b = (1 if i > 0 else 0), (1 if j > 0 else 0)
                runs = [(2 * a + b, 12 + 2 * (1 - a) + 1 - b, 1)]
            for src, dst, count in runs:
                n = len(moves)
                moves.append(pltpu.make_async_remote_copy(
                    src_ref=buf.at[pl.ds(src * rows, count * rows)],
                    dst_ref=buf.at[pl.ds(dst * rows, count * rows)],
                    send_sem=ssem.at[n], recv_sem=rsem.at[n],
                    device_id=peer(i, j), device_id_type=MESH))
                kinds[0 if j == 0 else 1 if i == 0 else 2].append(moves[-1])
        return kinds

    ox = ((gx * 2 + 1) * 2).astype(F32)
    oy = ((gy * 2 + 1) * 2).astype(F32)

    xt = [own[0] - ox, own[1] - oy, own[2] - 4.0]
    for k, value in enumerate(distance_rows(xt, False)):
        spread_rows(traw, k, 24, value)
    for t in range(8):
        p = t % 2
        both = jnp.concatenate([traw[(2 * t + h) * 24:(2 * t + h + 1) * 24, :] for h in range(2)], axis=1)
        both = jnp.concatenate([both, jnp.zeros((8, 256), F32)], axis=0).astype(BF16)
        blocks = [(BOTH[p][0], both), (BOTH[p][1], both), (ONE[p], both[:, LANE[p]:LANE[p] + 128])]
        near[t] = jnp.concatenate(
            [jnp.concatenate([b if ly == at else jnp.zeros_like(b) for ly in range(4)], axis=0) for at, b in blocks], axis=1)

    eye = (lax.broadcasted_iota(jnp.int32, (128, 128), 0) == lax.broadcasted_iota(jnp.int32, (128, 128), 1))
    eye16 = jnp.where(eye, 1.0, 0.0).astype(BF16)
    off[...] = jnp.where(eye, 0.0, 1.0)

    def source(first, count, inside):
        def chan(ch):
            return take_rows(ext, first * 8 + ch, 8, count)

        x = [chan(0) - ox, chan(1) - oy, chan(2) - 4.0]
        v = [chan(3 + d) for d in range(3)]
        w = chan(7)
        if inside is not None:
            w = jnp.where(inside, w, 0.0)
        return x, v, chan(6), w, [w * x[d] for d in range(3)], [w * v[d] for d in range(3)]

    def features(first, count, inside):
        x, v, r, w, wx, wv = source(first, count, inside)
        wr = w * r
        wp = w * power7(r + 1.0)
        zero = jnp.zeros_like(w)
        rows = [w] + wx + [wx[a] * x[b] for a in range(3) for b in range(a, 3)] + [wr] + [wr * x[d] for d in range(3)]
        rows += wv + [wv[0] * x[0] + wv[1] * x[1] + wv[2] * x[2]] + [wp] + [wp * x[d] for d in range(3)] + [zero, zero]
        for f, value in enumerate(rows + distance_rows(x, True)):
            spread_rows(raw, first * RAW + f, RAW, value)

    def features_d(first, count, inside):
        x, v, r, w, wx, wv = source(first, count, inside)
        zero = jnp.zeros_like(w)
        wvx = wv[0] * x[0] + wv[1] * x[1] + wv[2] * x[2]
        e, f = pieces(w), pieces(w * r)
        rows = wv + wx + [wx[a] * x[b] for a in range(3) for b in range(a, 3)]
        rows += [wv[a] * x[b] for a in range(3) for b in range(3)] + [wvx * x[d] for d in range(3)]
        rows += [e[0], f[0], e[1], f[1], e[2], f[2], zero, zero]
        for f, value in enumerate(rows):
            spread_rows(raw, first * RAW_D + f, RAW_D, value)

    def column(c):
        dist = []
        for cell in range(c * 4, c * 4 + 4):
            got = raw[cell * RAW:cell * RAW + RAW, :]
            feat_c[cell] = jnp.concatenate(list(pieces(got[0:24])) + [jnp.zeros((8, 128), F32)], axis=0).astype(BF16)
            dist += [got[24:48], jnp.zeros((8, 128), F32)]
        dist = jnp.concatenate(dist, axis=0).astype(BF16)
        far[c] = lax.dot_general(eye16, dist, (((1,), (1,)), ((), ())), preferred_element_type=F32).astype(BF16)

    def column_d(c):
        for cell in range(c * 4, c * 4 + 4):
            got = raw[cell * RAW_D:cell * RAW_D + RAW_D, :]
            feat_d[cell] = jnp.concatenate(list(pieces(got[0:24])) + [got[24:32]], axis=0).astype(BF16)

    def two(x):
        hi = x.astype(BF16)
        lo = (x - hi.astype(F32)).astype(BF16)
        return hi, lo

    def weigh(tc, p, col, full_c, half_c, full_d, half_d, self_col):
        lhs = far[col]
        for at in range(0, 640, WIDTH):
          for r in range(0, 128, ROWS):
            gap = jnp.dot(lhs[r:r + ROWS], near[tc * 2 + p, :, at:min(at + WIDTH, 640)], preferred_element_type=F32)
            d2 = jnp.maximum(gap, TINY)
            wedge = jnp.maximum(1.0 - d2 * lax.rsqrt(d2), 0.0)
            c = wedge * wedge * wedge
            d = c * pl.reciprocal(d2 + SOFT4, approx=True)
            k = at // 256
            if self_col and k < 2 and at <= 384 * k < at + WIDTH:
                parts_d = [d[:, j:j + 128] for j in range(0, d.shape[1], 128)]
                parts_d[(384 * k - at) // 128] *= off[r:r + ROWS]
                d = jnp.concatenate(parts_d, axis=1)
            lane = at % 256
            for (hi, lo), full, half in ((two(c), full_c, half_c), (two(d), full_d, half_d)):
                out = full.at[k * 256:k * 256 + 256, lane:lane + gap.shape[1]] if k < 2 else half
                out[r:r + ROWS] = hi
                out[128 + r:128 + r + ROWS] = lo

    def total(feat, rows, p, cols, full, half):
        lf, lh = [], []
        for c in cols:
            for ly in BOTH[p]:
                lf += [feat[c * 4 + ly]] * 2
            lh += [feat[c * 4 + ONE[p]]] * 2
        n = len(cols)
        f = jnp.dot(jnp.concatenate(lf, axis=1), full.reshape(n * 512, 256), preferred_element_type=F32)
        h = jnp.dot(jnp.concatenate(lh, axis=1), half.reshape(n * 256, 128), preferred_element_type=F32)
        return (f[:, 0:128], f[:, 128:256] + h) if p == 0 else (f[:, 0:128] + h, f[:, 128:256])

    def mates(tc):
        return [(tc + k) % 4 for k in range(4)]

    def halo(tc):
        a, b = tc // 2, tc % 2
        return [4 + 2 * a, 5 + 2 * a, 8 + 2 * b, 9 + 2 * b, 12 + tc]

    def fold(s):
        return s[0:24] + s[24:48] + s[48:72]

    features(0, 16, None)
    for c in range(4):
        column(c)

    def own_weights(tc):
        for p in range(2):
            cols = mates(tc)
            for k in range(4):
                weigh(tc, p, cols[k], cfull.at[p, tc, k], chalf.at[p, tc, k], dfull.at[p, tc, k], dhalf.at[p, tc, k], k == 0)

    def own_sums(tc):
        for p in range(2):
            got = total(feat_c, 80, p, mates(tc), cfull[p, tc, 0:4], chalf[p, tc, 0:4])
            for h in range(2):
                sums[tc * 2 + p, h] = got[h]

    for tc in range(CUT):
        own_weights(tc)
    if comm:
        pl.semaphore_wait(barrier, 8)
        moves = swap(ext, 32, send_sem, recv_sem)
        for c in moves[2] + moves[1] + moves[0]:
            c.start()
    for tc in range(CUT, 4):
        own_weights(tc)
    for tc in range(4):
        own_sums(tc)
    cell = lax.broadcasted_iota(jnp.int32, (48, 128), 0) // 4 + 4
    pair_of = cell // 2
    below_a = (pair_of == 2) | (cell == 12) | (cell == 13)
    above_a = (pair_of == 3) | (cell == 14) | (cell == 15)
    below_b = (pair_of == 4) | (cell == 12) | (cell == 14)
    above_b = (pair_of == 5) | (cell == 13) | (cell == 15)
    outside = (below_a & (gx == 0)) | (above_a & (gx == nx - 1)) | (below_b & (gy == 0)) | (above_b & (gy == ny - 1))
    inside = jnp.logical_not(outside)

    def halo_pairs(group, slots):
        if comm:
            for c in moves[group]:
                c.wait()
        first = 4 + 4 * group
        features(first * 4, 16, inside[16 * group:16 * group + 16])
        for c in range(first, first + 4):
            column(c)
        for tc in range(4):
            for p in range(2):
                cols = halo(tc)
                for k in slots:
                    weigh(tc, p, cols[k], cfull.at[p, tc, 4 + k], chalf.at[p, tc, 4 + k], dfull.at[p, tc, 4 + k],
                          dhalf.at[p, tc, 4 + k], False)

    halo_pairs(0, (0, 1))
    for tc in range(4):
        for p in range(2):
            got = total(feat_c, 80, p, halo(tc)[0:2], cfull[p, tc, 4:6], chalf[p, tc, 4:6])
            for h in range(2):
                sums[tc * 2 + p, h] += got[h]
    halo_pairs(1, (2, 3))
    halo_pairs(2, (4,))
    for tc in range(4):
        for p in range(2):
            got = total(feat_c, 80, p, halo(tc)[2:5], cfull[p, tc, 6:9], chalf[p, tc, 6:9])
            for h in range(2):
                base = (tc * 4 + p * 2 + h) * 56
                parts[base:base + 24, :] = fold(sums[tc * 2 + p, h] + got[h])

    def part(f, stride=56):
        return take_rows(parts, f, stride, 16)

    def dot3(a, b):
        return a[0] * b[0] + a[1] * b[1] + a[2] * b[2]

    pc = [part(f) for f in range(22)]
    s0, s1, sr, srx, sv, svx, sp, spx = pc[0], pc[1:4], pc[10], pc[11:14], pc[14:17], pc[17], pc[18], pc[19:22]
    pair = {}
    n = 0
    for a in range(3):
        for b in range(a, 3):
            pair[a, b] = pair[b, a] = n
            n += 1
    mom = {}
    for a in range(3):
        for b in range(a, 3):
            m = -(pc[4 + pair[a, b]] - xt[a] * s1[b] - xt[b] * (s1[a] - xt[a] * s0))
            mom[a, b] = m + FLOOR if a == b else m
    rt = own[6]
    back = [s0 * xt[a] - s1[a] for a in range(3)]
    slope = [(sr * xt[a] - srx[a]) - rt * back[a] for a in range(3)]
    m00, m01, m02, m11, m12, m22 = mom[0, 0], mom[0, 1], mom[0, 2], mom[1, 1], mom[1, 2], mom[2, 2]
    c00 = m11 * m22 - m12 * m12
    c01 = m02 * m12 - m01 * m22
    c02 = m01 * m12 - m02 * m11
    c11 = m00 * m22 - m02 * m02
    c12 = m01 * m02 - m00 * m12
    c22 = m00 * m11 - m01 * m01
    det = m00 * c00 + m01 * c01 + m02 * c02
    grad = [(c00 * slope[0] + c01 * slope[1] + c02 * slope[2]) / det,
            (c01 * slope[0] + c11 * slope[1] + c12 * slope[2]) / det,
            (c02 * slope[0] + c12 * slope[1] + c22 * slope[2]) / det]

    for d in range(3):
        spread_rows(gext, d, 4, grad[d])
    if comm:
        moves = swap(gext, 16, gsend_sem, grecv_sem)
        for c in moves[2] + moves[1] + moves[0]:
            c.start()

    features_d(0, 16, None)
    features_d(16, 48, inside)
    for c in range(16):
        column_d(c)

    for tc in range(4):
        for p in range(2):
            mine = total(feat_d, 80, p, mates(tc), dfull[p, tc, 0:4], dhalf[p, tc, 0:4])
            got = total(feat_d, 80, p, halo(tc), dfull[p, tc, 4:9], dhalf[p, tc, 4:9])
            for h in range(2):
                s = mine[h] + got[h]
                base = (tc * 4 + p * 2 + h) * 56
                parts[pl.ds(base + 24, 24), :] = fold(s)
                parts[pl.ds(base + 48, 8), :] = s[72:80]

    def slopes(first, count, inside):
        x = [take_rows(ext, first * 8 + d, 8, count) - o for d, o in enumerate((ox, oy, 4.0))]
        w = take_rows(ext, first * 8 + 7, 8, count)
        if inside is not None:
            w = jnp.where(inside, w, 0.0)
        g = [take_rows(gext, first * 4 + d, 4, count) for d in range(3)]
        rows = [pieces(w * g[d]) for d in range(3)] + [pieces(w * dot3(g, x))]
        for k in range(3):
            for f in range(4):
                spread_rows(raw, first * 16 + k * 4 + f, 16, rows[f][k])
        for f in range(12, 16):
            spread_rows(raw, first * 16 + f, 16, jnp.zeros_like(w))
        for n in range(first, first + count):
            feat_g[n] = raw[n * 16:n * 16 + 16, :].astype(BF16)

    slopes(0, 16, None)

    for tc in range(4):
        for p in range(2):
            got = total(feat_g, 16, p, mates(tc), cfull[p, tc, 0:4], chalf[p, tc, 0:4])
            for h in range(2):
                gsums[tc * 2 + p, h] = got[h]

    vt = own[3:6]
    pt = power7(rho)
    vtx = dot3(vt, xt)
    flow = dot3(sv, xt) - svx - vtx * s0 + dot3(vt, s1)
    pd = [part(24 + f) for f in range(30)]
    d0 = pd[24] + pd[26] + pd[28]
    dr = pd[25] + pd[27] + pd[29]
    dv, d1, dxx, dvx, dvxx = pd[0:3], pd[3:6], pd[6:12], [pd[12:15], pd[15:18], pd[18:21]], pd[21:24]
    spread = -2.0 * ((sr - rt * s0) - SOFT4 * (dr - rt * d0))
    trace = dvx[0][0] + dvx[1][1] + dvx[2][2]
    head = dot3(dv, xt) - trace - vtx * d0 + dot3(vt, d1)
    push = []
    for b in range(3):
        tail = (xt[0] * dvx[0][b] + xt[1] * dvx[1][b] + xt[2] * dvx[2][b] - dvxx[b] - vtx * d1[b]
                + vt[0] * dxx[pair[0, b]] + vt[1] * dxx[pair[1, b]] + vt[2] * dxx[pair[2, b]])
        push.append(-(pt * back[b] + (sp * xt[b] - spx[b])) - (0.25 * ALPHA_SOUND) * (xt[b] * head - tail))
    moving = kind == 1
    for b in range(3):
        force = push[b] / rho - (GRAVITY if b == 2 else 0.0)
        acc_ref[b] = jnp.where(moving, force, 0.0)
    spread = spread - dot3(grad, back)

    for group, (lo, hi) in enumerate(((0, 2), (2, 4), (4, 5))):
        if comm:
            for c in moves[group]:
                c.wait()
        slopes(16 + 16 * group, 16, inside[16 * group:16 * group + 16])
        for tc in range(4):
            for p in range(2):
                got = total(feat_g, 16, p, halo(tc)[lo:hi], cfull[p, tc, 4 + lo:4 + hi], chalf[p, tc, 4 + lo:4 + hi])
                for h in range(2):
                    if group < 2:
                        gsums[tc * 2 + p, h] += got[h]
                    else:
                        base = (tc * 4 + p * 2 + h) * 16
                        parts[base:base + 16, :] = gsums[tc * 2 + p, h] + got[h]

    q = [part(f, 16) for f in range(12)]
    q = [q[f] + q[f + 4] + q[f + 8] for f in range(4)]
    spread = spread - (dot3(q, xt) - q[3])
    rate = -rho * flow + DELTA_SOUND * spread
    rate_ref[...] = jnp.where(kind > 0, rate, 0.0)


def last(a_ref, b_ref, rate_ref, acc_ref):
    rate_ref[...] = a_ref[...]
    acc_ref[...] = b_ref[...]


def finish(rate, acc):
    vmem = pl.BlockSpec(memory_space=pltpu.VMEM)
    return pl.pallas_call(
        last,
        out_shape=(jax.ShapeDtypeStruct((16, 128), F32), jax.ShapeDtypeStruct((3, 16, 128), F32)),
        in_specs=[vmem, vmem],
        out_specs=(vmem, vmem),
    )(rate, acc)


def local(comm, positions, velocity, density, mass, kind):
    vmem = pl.BlockSpec(memory_space=pltpu.VMEM)
    dma = pltpu.SemaphoreType.DMA
    rate, acc = pl.pallas_call(
        functools.partial(kernel, comm),
        out_shape=(jax.ShapeDtypeStruct((16, 128), F32), jax.ShapeDtypeStruct((3, 16, 128), F32)),
        in_specs=[vmem] * 5,
        out_specs=(vmem, vmem),
        scratch_shapes=[
            pltpu.VMEM((512, 128), F32),
            pltpu.VMEM((256, 128), F32),
            pltpu.VMEM((64 * RAW, 128), F32),
            pltpu.VMEM((16 * 24, 128), F32),
            pltpu.VMEM((64, 80, 128), BF16),
            pltpu.VMEM((64, 80, 128), BF16),
            pltpu.VMEM((64, 16, 128), BF16),
            pltpu.VMEM((16, 128, 128), BF16),
            pltpu.VMEM((8, 128, 640), BF16),
            pltpu.VMEM((2, 4, 9, 512, 256), BF16),
            pltpu.VMEM((2, 4, 9, 256, 128), BF16),
            pltpu.VMEM((2, 4, 9, 512, 256), BF16),
            pltpu.VMEM((2, 4, 9, 256, 128), BF16),
            pltpu.VMEM((8, 2, 80, 128), F32),
            pltpu.VMEM((16 * 56, 128), F32),
            pltpu.VMEM((8, 2, 16, 128), F32),
            pltpu.VMEM((128, 128), F32),
            dma((10,)), dma((10,)), dma((10,)), dma((10,)),
        ],
        compiler_params=pltpu.CompilerParams(
            vmem_limit_bytes=63 * 1024 * 1024,
            **(dict(collective_id=0, has_side_effects=True) if comm else {})),
        cost_estimate=pl.CostEstimate(flops=2 * 10**9, bytes_accessed=10**6, transcendentals=10**7),
    )(positions.reshape(3, 16, 128), velocity.reshape(3, 16, 128), density.reshape(16, 128),
      mass.reshape(16, 128), kind.reshape(16, 128))
    rate, acc = finish(rate, acc)
    return rate.reshape(2, 2, 4, 128), acc.reshape(3, 2, 2, 4, 128)


def solution(mesh):
    in_specs = (
        P(None, "gx", "gy", None, None),
        P(None, "gx", "gy", None, None),
        P("gx", "gy", None, None),
        P("gx", "gy", None, None),
        P("gx", "gy", None, None),
    )
    out_specs = (P("gx", "gy", None, None), P(None, "gx", "gy", None, None))
    return jax.shard_map(functools.partial(local, True), mesh=mesh, in_specs=in_specs, out_specs=out_specs,
                         check_vma=False)
```

```python
import functools
import math

import jax
import jax.numpy as jnp
from jax import lax
from jax.experimental import pallas as pl
from jax.experimental.pallas import tpu as pltpu
from jax.sharding import PartitionSpec as P

MESH = pl.DeviceIdType.MESH
KERNEL_NORM = 21.0 / (16.0 * math.pi)
SCALE = -5.0 * KERNEL_NORM
STIFF = 9.0 / 7.0
DELTA_SOUND = 0.3
ALPHA_SOUND = 0.3
FLOOR = 0.25
GRAVITY = 1.0
SOFT4 = 0.0025

F32 = jnp.float32
BF16 = jnp.bfloat16
RAW = 48
RAW_D = 32
SIDES = [(i, j) for i in (-1, 0, 1) for j in (-1, 0, 1) if (i, j) != (0, 0)]
TINY = 1e-12
BOTH = {0: (0, 1), 1: (2, 3)}
ONE = {0: 2, 1: 1}
LANE = {0: 128, 1: 0}
CUT = 2
WIDTH = 256
ROWS = 128


def pieces(x):
    a = x.astype(BF16).astype(F32)
    r = x - a
    b = r.astype(BF16).astype(F32)
    return a, b, r - b


def power7(r):
    r2 = r * r
    r4 = r2 * r2
    return STIFF * (r4 * r2 * r - 1.0)


def distance_rows(xs, source):
    half = [0.5 * x for x in xs]
    cut = [pieces(h) for h in half]
    norm = pieces(half[0] * half[0] + half[1] * half[1] + half[2] * half[2])
    one = jnp.ones_like(half[0])
    rows = []
    for i in range(3):
        for j in range(3 - i):
            for d in range(3):
                rows.append(-2.0 * cut[d][i] if source else cut[d][j])
    rows += list(norm) + [one] * 3 if source else [one] * 3 + list(norm)
    return rows


def kernel(comm, pos_ref, vel_ref, rho_ref, mass_ref, kind_ref, rate_ref, acc_ref,
           ext, gext, raw, traw, feat_c, feat_d, feat_g, far, near, cfull, chalf, dfull, dhalf, sums, parts, gsums, off,
           send_sem, recv_sem, gsend_sem, grecv_sem):
    if comm:
        gx = lax.axis_index("gx")
        gy = lax.axis_index("gy")
        nx = lax.axis_size("gx")
        ny = lax.axis_size("gy")
    else:
        gx, gy, nx, ny = jnp.int32(1), jnp.int32(1), 16, 16

    def peer(i, j):
        return (lax.rem(gx + i + nx, nx), lax.rem(gy + j + ny, ny))

    if comm:
        barrier = pltpu.get_barrier_semaphore()
        for i, j in SIDES:
            pl.semaphore_signal(barrier, inc=1, device_id=peer(i, j), device_id_type=MESH)

    kind = kind_ref[...]
    rho = rho_ref[...]
    vol = jnp.where(kind > 0, mass_ref[...], 0.0) / rho * SCALE
    own = [pos_ref[0], pos_ref[1], pos_ref[2], vel_ref[0], vel_ref[1], vel_ref[2], rho - 1.0, vol]

    def spread_rows(buf, start, stride, value):
        for h in range(value.shape[0] // 8):
            buf[pl.ds(start + h * 8 * stride, 8, stride=stride), :] = value[h * 8:h * 8 + 8]

    def take_rows(buf, start, stride, count):
        return jnp.concatenate([buf[pl.ds(start + h * 8 * stride, 8, stride=stride), :] for h in range(count // 8)], axis=0)

    for ch in range(8):
        spread_rows(ext, ch, 8, own[ch])

    def swap(buf, rows, ssem, rsem):
        moves = []
        kinds = ([], [], [])
        for i, j in SIDES:
            if j == 0:
                a = 1 if i > 0 else 0
                runs = [(2 * a, 4 + 2 * (1 - a), 2)]
            elif i == 0:
                b = 1 if j > 0 else 0
                runs = [(2 * a + b, 8 + 2 * (1 - b) + a, 1) for a in range(2)]
            else:
                a, b = (1 if i > 0 else 0), (1 if j > 0 else 0)
                runs = [(2 * a + b, 12 + 2 * (1 - a) + 1 - b, 1)]
            for src, dst, count in runs:
                n = len(moves)
                moves.append(pltpu.make_async_remote_copy(
                    src_ref=buf.at[pl.ds(src * rows, count * rows)],
                    dst_ref=buf.at[pl.ds(dst * rows, count * rows)],
                    send_sem=ssem.at[n], recv_sem=rsem.at[n],
                    device_id=peer(i, j), device_id_type=MESH))
                kinds[0 if j == 0 else 1 if i == 0 else 2].append(moves[-1])
        return kinds

    ox = ((gx * 2 + 1) * 2).astype(F32)
    oy = ((gy * 2 + 1) * 2).astype(F32)

    xt = [own[0] - ox, own[1] - oy, own[2] - 4.0]
    for k, value in enumerate(distance_rows(xt, False)):
        spread_rows(traw, k, 24, value)
    for t in range(8):
        p = t % 2
        both = jnp.concatenate([traw[(2 * t + h) * 24:(2 * t + h + 1) * 24, :] for h in range(2)], axis=1)
        both = jnp.concatenate([both, jnp.zeros((8, 256), F32)], axis=0).astype(BF16)
        blocks = [(BOTH[p][0], both), (BOTH[p][1], both), (ONE[p], both[:, LANE[p]:LANE[p] + 128])]
        near[t] = jnp.concatenate(
            [jnp.concatenate([b if ly == at else jnp.zeros_like(b) for ly in range(4)], axis=0) for at, b in blocks], axis=1)

    eye = (lax.broadcasted_iota(jnp.int32, (128, 128), 0) == lax.broadcasted_iota(jnp.int32, (128, 128), 1))
    eye16 = jnp.where(eye, 1.0, 0.0).astype(BF16)
    off[...] = jnp.where(eye, 0.0, 1.0)

    def source(first, count, inside):
        def chan(ch):
            return take_rows(ext, first * 8 + ch, 8, count)

        x = [chan(0) - ox, chan(1) - oy, chan(2) - 4.0]
        v = [chan(3 + d) for d in range(3)]
        w = chan(7)
        if inside is not None:
            w = jnp.where(inside, w, 0.0)
        return x, v, chan(6), w, [w * x[d] for d in range(3)], [w * v[d] for d in range(3)]

    def features(first, count, inside):
        x, v, r, w, wx, wv = source(first, count, inside)
        wr = w * r
        wp = w * power7(r + 1.0)
        zero = jnp.zeros_like(w)
        rows = [w] + wx + [wx[a] * x[b] for a in range(3) for b in range(a, 3)] + [wr] + [wr * x[d] for d in range(3)]
        rows += wv + [wv[0] * x[0] + wv[1] * x[1] + wv[2] * x[2]] + [wp] + [wp * x[d] for d in range(3)] + [zero, zero]
        for f, value in enumerate(rows + distance_rows(x, True)):
            spread_rows(raw, first * RAW + f, RAW, value)

    def features_d(first, count, inside):
        x, v, r, w, wx, wv = source(first, count, inside)
        zero = jnp.zeros_like(w)
        wvx = wv[0] * x[0] + wv[1] * x[1] + wv[2] * x[2]
        e, f = pieces(w), pieces(w * r)
        rows = wv + wx + [wx[a] * x[b] for a in range(3) for b in range(a, 3)]
        rows += [wv[a] * x[b] for a in range(3) for b in range(3)] + [wvx * x[d] for d in range(3)]
        rows += [e[0], f[0], e[1], f[1], e[2], f[2], zero, zero]
        for f, value in enumerate(rows):
            spread_rows(raw, first * RAW_D + f, RAW_D, value)

    def column(c):
        dist = []
        for cell in range(c * 4, c * 4 + 4):
            got = raw[cell * RAW:cell * RAW + RAW, :]
            feat_c[cell] = jnp.concatenate(list(pieces(got[0:24])) + [jnp.zeros((8, 128), F32)], axis=0).astype(BF16)
            dist += [got[24:48], jnp.zeros((8, 128), F32)]
        dist = jnp.concatenate(dist, axis=0).astype(BF16)
        far[c] = lax.dot_general(eye16, dist, (((1,), (1,)), ((), ())), preferred_element_type=F32).astype(BF16)

    def column_d(c):
        for cell in range(c * 4, c * 4 + 4):
            got = raw[cell * RAW_D:cell * RAW_D + RAW_D, :]
            feat_d[cell] = jnp.concatenate(list(pieces(got[0:24])) + [got[24:32]], axis=0).astype(BF16)

    def two(x):
        hi = x.astype(BF16)
        lo = (x - hi.astype(F32)).astype(BF16)
        return hi, lo

    def weigh(tc, p, col, full_c, half_c, full_d, half_d, self_col):
        lhs = far[col]
        for at in range(0, 640, WIDTH):
          for r in range(0, 128, ROWS):
            gap = jnp.dot(lhs[r:r + ROWS], near[tc * 2 + p, :, at:min(at + WIDTH, 640)], preferred_element_type=F32)
            d2 = jnp.maximum(gap, TINY)
            wedge = jnp.maximum(1.0 - d2 * lax.rsqrt(d2), 0.0)
            c = wedge * wedge * wedge
            d = c * pl.reciprocal(d2 + SOFT4, approx=True)
            k = at // 256
            if self_col and k < 2 and at <= 384 * k < at + WIDTH:
                parts_d = [d[:, j:j + 128] for j in range(0, d.shape[1], 128)]
                parts_d[(384 * k - at) // 128] *= off[r:r + ROWS]
                d = jnp.concatenate(parts_d, axis=1)
            lane = at % 256
            for (hi, lo), full, half in ((two(c), full_c, half_c), (two(d), full_d, half_d)):
                out = full.at[k * 256:k * 256 + 256, lane:lane + gap.shape[1]] if k < 2 else half
                out[r:r + ROWS] = hi
                out[128 + r:128 + r + ROWS] = lo

    def total(feat, rows, p, cols, full, half):
        lf, lh = [], []
        for c in cols:
            for ly in BOTH[p]:
                lf += [feat[c * 4 + ly]] * 2
            lh += [feat[c * 4 + ONE[p]]] * 2
        n = len(cols)
        f = jnp.dot(jnp.concatenate(lf, axis=1), full.reshape(n * 512, 256), preferred_element_type=F32)
        h = jnp.dot(jnp.concatenate(lh, axis=1), half.reshape(n * 256, 128), preferred_element_type=F32)
        return (f[:, 0:128], f[:, 128:256] + h) if p == 0 else (f[:, 0:128] + h, f[:, 128:256])

    def mates(tc):
        return [(tc + k) % 4 for k in range(4)]

    def halo(tc):
        a, b = tc // 2, tc % 2
        return [4 + 2 * a, 5 + 2 * a, 8 + 2 * b, 9 + 2 * b, 12 + tc]

    def fold(s):
        return s[0:24] + s[24:48] + s[48:72]

    features(0, 16, None)
    for c in range(4):
        column(c)

    def own_weights(tc):
        for p in range(2):
            cols = mates(tc)
            for k in range(4):
                weigh(tc, p, cols[k], cfull.at[p, tc, k], chalf.at[p, tc, k], dfull.at[p, tc, k], dhalf.at[p, tc, k], k == 0)

    def own_sums(tc):
        for p in range(2):
            got = total(feat_c, 80, p, mates(tc), cfull[p, tc, 0:4], chalf[p, tc, 0:4])
            for h in range(2):
                sums[tc * 2 + p, h] = got[h]

    for tc in range(CUT):
        own_weights(tc)
    if comm:
        pl.semaphore_wait(barrier, 8)
        moves = swap(ext, 32, send_sem, recv_sem)
        for c in moves[2] + moves[1] + moves[0]:
            c.start()
    for tc in range(CUT, 4):
        own_weights(tc)
    for tc in range(4):
        own_sums(tc)
    cell = lax.broadcasted_iota(jnp.int32, (48, 128), 0) // 4 + 4
    pair_of = cell // 2
    below_a = (pair_of == 2) | (cell == 12) | (cell == 13)
    above_a = (pair_of == 3) | (cell == 14) | (cell == 15)
    below_b = (pair_of == 4) | (cell == 12) | (cell == 14)
    above_b = (pair_of == 5) | (cell == 13) | (cell == 15)
    outside = (below_a & (gx == 0)) | (above_a & (gx == nx - 1)) | (below_b & (gy == 0)) | (above_b & (gy == ny - 1))
    inside = jnp.logical_not(outside)

    def halo_pairs(group, slots):
        if comm:
            for c in moves[group]:
                c.wait()
        first = 4 + 4 * group
        features(first * 4, 16, inside[16 * group:16 * group + 16])
        for c in range(first, first + 4):
            column(c)
        for tc in range(4):
            for p in range(2):
                cols = halo(tc)
                for k in slots:
                    weigh(tc, p, cols[k], cfull.at[p, tc, 4 + k], chalf.at[p, tc, 4 + k], dfull.at[p, tc, 4 + k],
                          dhalf.at[p, tc, 4 + k], False)

    halo_pairs(0, (0, 1))
    halo_pairs(1, (2, 3))
    halo_pairs(2, (4,))
    for tc in range(4):
        for p in range(2):
            got = total(feat_c, 80, p, halo(tc), cfull[p, tc, 4:9], chalf[p, tc, 4:9])
            for h in range(2):
                base = (tc * 4 + p * 2 + h) * 56
                parts[base:base + 24, :] = fold(sums[tc * 2 + p, h] + got[h])

    def part(f, stride=56):
        return take_rows(parts, f, stride, 16)

    def dot3(a, b):
        return a[0] * b[0] + a[1] * b[1] + a[2] * b[2]

    pc = [part(f) for f in range(22)]
    s0, s1, sr, srx, sv, svx, sp, spx = pc[0], pc[1:4], pc[10], pc[11:14], pc[14:17], pc[17], pc[18], pc[19:22]
    pair = {}
    n = 0
    for a in range(3):
        for b in range(a, 3):
            pair[a, b] = pair[b, a] = n
            n += 1
    mom = {}
    for a in range(3):
        for b in range(a, 3):
            m = -(pc[4 + pair[a, b]] - xt[a] * s1[b] - xt[b] * (s1[a] - xt[a] * s0))
            mom[a, b] = m + FLOOR if a == b else m
    rt = own[6]
    back = [s0 * xt[a] - s1[a] for a in range(3)]
    slope = [(sr * xt[a] - srx[a]) - rt * back[a] for a in range(3)]
    m00, m01, m02, m11, m12, m22 = mom[0, 0], mom[0, 1], mom[0, 2], mom[1, 1], mom[1, 2], mom[2, 2]
    c00 = m11 * m22 - m12 * m12
    c01 = m02 * m12 - m01 * m22
    c02 = m01 * m12 - m02 * m11
    c11 = m00 * m22 - m02 * m02
    c12 = m01 * m02 - m00 * m12
    c22 = m00 * m11 - m01 * m01
    det = m00 * c00 + m01 * c01 + m02 * c02
    grad = [(c00 * slope[0] + c01 * slope[1] + c02 * slope[2]) / det,
            (c01 * slope[0] + c11 * slope[1] + c12 * slope[2]) / det,
            (c02 * slope[0] + c12 * slope[1] + c22 * slope[2]) / det]

    for d in range(3):
        spread_rows(gext, d, 4, grad[d])
    if comm:
        moves = swap(gext, 16, gsend_sem, grecv_sem)
        for c in moves[2] + moves[1] + moves[0]:
            c.start()

    features_d(0, 16, None)
    features_d(16, 48, inside)
    for c in range(16):
        column_d(c)

    for tc in range(4):
        for p in range(2):
            mine = total(feat_d, 80, p, mates(tc), dfull[p, tc, 0:4], dhalf[p, tc, 0:4])
            got = total(feat_d, 80, p, halo(tc), dfull[p, tc, 4:9], dhalf[p, tc, 4:9])
            for h in range(2):
                s = mine[h] + got[h]
                base = (tc * 4 + p * 2 + h) * 56
                parts[pl.ds(base + 24, 24), :] = fold(s)
                parts[pl.ds(base + 48, 8), :] = s[72:80]

    def slopes(first, count, inside):
        x = [take_rows(ext, first * 8 + d, 8, count) - o for d, o in enumerate((ox, oy, 4.0))]
        w = take_rows(ext, first * 8 + 7, 8, count)
        if inside is not None:
            w = jnp.where(inside, w, 0.0)
        g = [take_rows(gext, first * 4 + d, 4, count) for d in range(3)]
        rows = [pieces(w * g[d]) for d in range(3)] + [pieces(w * dot3(g, x))]
        for k in range(3):
            for f in range(4):
                spread_rows(raw, first * 16 + k * 4 + f, 16, rows[f][k])
        for f in range(12, 16):
            spread_rows(raw, first * 16 + f, 16, jnp.zeros_like(w))
        for n in range(first, first + count):
            feat_g[n] = raw[n * 16:n * 16 + 16, :].astype(BF16)

    slopes(0, 16, None)

    for tc in range(4):
        for p in range(2):
            got = total(feat_g, 16, p, mates(tc), cfull[p, tc, 0:4], chalf[p, tc, 0:4])
            for h in range(2):
                gsums[tc * 2 + p, h] = got[h]

    vt = own[3:6]
    pt = power7(rho)
    vtx = dot3(vt, xt)
    flow = dot3(sv, xt) - svx - vtx * s0 + dot3(vt, s1)
    pd = [part(24 + f) for f in range(30)]
    d0 = pd[24] + pd[26] + pd[28]
    dr = pd[25] + pd[27] + pd[29]
    dv, d1, dxx, dvx, dvxx = pd[0:3], pd[3:6], pd[6:12], [pd[12:15], pd[15:18], pd[18:21]], pd[21:24]
    spread = -2.0 * ((sr - rt * s0) - SOFT4 * (dr - rt * d0))
    trace = dvx[0][0] + dvx[1][1] + dvx[2][2]
    head = dot3(dv, xt) - trace - vtx * d0 + dot3(vt, d1)
    push = []
    for b in range(3):
        tail = (xt[0] * dvx[0][b] + xt[1] * dvx[1][b] + xt[2] * dvx[2][b] - dvxx[b] - vtx * d1[b]
                + vt[0] * dxx[pair[0, b]] + vt[1] * dxx[pair[1, b]] + vt[2] * dxx[pair[2, b]])
        push.append(-(pt * back[b] + (sp * xt[b] - spx[b])) - (0.25 * ALPHA_SOUND) * (xt[b] * head - tail))
    moving = kind == 1
    for b in range(3):
        force = push[b] / rho - (GRAVITY if b == 2 else 0.0)
        acc_ref[b] = jnp.where(moving, force, 0.0)
    spread = spread - dot3(grad, back)

    for group, (lo, hi) in enumerate(((0, 2), (2, 4), (4, 5))):
        if comm:
            for c in moves[group]:
                c.wait()
        slopes(16 + 16 * group, 16, inside[16 * group:16 * group + 16])
        for tc in range(4):
            for p in range(2):
                got = total(feat_g, 16, p, halo(tc)[lo:hi], cfull[p, tc, 4 + lo:4 + hi], chalf[p, tc, 4 + lo:4 + hi])
                for h in range(2):
                    if group < 2:
                        gsums[tc * 2 + p, h] += got[h]
                    else:
                        base = (tc * 4 + p * 2 + h) * 16
                        parts[base:base + 16, :] = gsums[tc * 2 + p, h] + got[h]

    q = [part(f, 16) for f in range(12)]
    q = [q[f] + q[f + 4] + q[f + 8] for f in range(4)]
    spread = spread - (dot3(q, xt) - q[3])
    rate = -rho * flow + DELTA_SOUND * spread
    rate_ref[...] = jnp.where(kind > 0, rate, 0.0)


def last(a_ref, b_ref, rate_ref, acc_ref):
    rate_ref[...] = a_ref[...]
    acc_ref[...] = b_ref[...]


def finish(rate, acc):
    vmem = pl.BlockSpec(memory_space=pltpu.VMEM)
    return pl.pallas_call(
        last,
        out_shape=(jax.ShapeDtypeStruct((16, 128), F32), jax.ShapeDtypeStruct((3, 16, 128), F32)),
        in_specs=[vmem, vmem],
        out_specs=(vmem, vmem),
    )(rate, acc)


def local(comm, positions, velocity, density, mass, kind):
    vmem = pl.BlockSpec(memory_space=pltpu.VMEM)
    dma = pltpu.SemaphoreType.DMA
    rate, acc = pl.pallas_call(
        functools.partial(kernel, comm),
        out_shape=(jax.ShapeDtypeStruct((16, 128), F32), jax.ShapeDtypeStruct((3, 16, 128), F32)),
        in_specs=[vmem] * 5,
        out_specs=(vmem, vmem),
        scratch_shapes=[
            pltpu.VMEM((512, 128), F32),
            pltpu.VMEM((256, 128), F32),
            pltpu.VMEM((64 * RAW, 128), F32),
            pltpu.VMEM((16 * 24, 128), F32),
            pltpu.VMEM((64, 80, 128), BF16),
            pltpu.VMEM((64, 80, 128), BF16),
            pltpu.VMEM((64, 16, 128), BF16),
            pltpu.VMEM((16, 128, 128), BF16),
            pltpu.VMEM((8, 128, 640), BF16),
            pltpu.VMEM((2, 4, 9, 512, 256), BF16),
            pltpu.VMEM((2, 4, 9, 256, 128), BF16),
            pltpu.VMEM((2, 4, 9, 512, 256), BF16),
            pltpu.VMEM((2, 4, 9, 256, 128), BF16),
            pltpu.VMEM((8, 2, 80, 128), F32),
            pltpu.VMEM((16 * 56, 128), F32),
            pltpu.VMEM((8, 2, 16, 128), F32),
            pltpu.VMEM((128, 128), F32),
            dma((10,)), dma((10,)), dma((10,)), dma((10,)),
        ],
        compiler_params=pltpu.CompilerParams(
            vmem_limit_bytes=63 * 1024 * 1024,
            **(dict(collective_id=0, has_side_effects=True) if comm else {})),
        cost_estimate=pl.CostEstimate(flops=2 * 10**9, bytes_accessed=10**6, transcendentals=10**7),
    )(positions.reshape(3, 16, 128), velocity.reshape(3, 16, 128), density.reshape(16, 128),
      mass.reshape(16, 128), kind.reshape(16, 128))
    rate, acc = finish(rate, acc)
    return rate.reshape(2, 2, 4, 128), acc.reshape(3, 2, 2, 4, 128)


def solution(mesh):
    in_specs = (
        P(None, "gx", "gy", None, None),
        P(None, "gx", "gy", None, None),
        P("gx", "gy", None, None),
        P("gx", "gy", None, None),
        P("gx", "gy", None, None),
    )
    out_specs = (P("gx", "gy", None, None), P(None, "gx", "gy", None, None))
    return jax.shard_map(functools.partial(local, True), mesh=mesh, in_specs=in_specs, out_specs=out_specs,
                         check_vma=False)
```
